128 devices in a mesh: blk: 32 (over y, z, x_lo), rep: 4 (over x_hi, core).
Axes of the slice: x: 4 (x_hi: 2, x_lo: 2; x = x_hi * 2 + x_lo), y: 4, z: 4, core: 2. Of those that a mesh axis runs over, the one named last changes fastest.
Arguments:
- features: bfloat16 [65536, 128], P('blk'), may hold values from -6 to 6
- node_order: int32 [32, 2048], P('blk'), may hold values from 0 to 2047, each once within a row
- adj_values: bfloat16 [32, 4, 8, 80, 128, 128], P('blk', 'rep'), may hold values from -0.0625 to 0.0625
- adj_rows: int32 [32, 4, 8, 80], P('blk', 'rep'), may hold values from 0 to 15, as said below
- adj_cols: int32 [32, 4, 8, 80], P('blk', 'rep'), may hold values from 0 to 15
- tile_count: int32 [32, 4, 8], P('blk', 'rep'), may hold values from 1 to 80, as said below
- weight: bfloat16 [128, 256], replicated, may hold values from -0.5 to 0.5
- upstream: bfloat16 [65536, 256], P(('blk', 'rep')), may hold values from -6 to 6
Outputs:
- activations: bfloat16 [65536, 256], P(('blk', 'rep'))
- grad_weight: float32 [128, 256], replicated
- grad_features: bfloat16 [65536, 128], P(('blk', 'rep'))
The draws below stay inside these ranges and needn't reach their ends.
Inputs may be any that keep to these rules, and one draw needn't show every extreme that they name: Within each slot of a device the pairs (adj_rows, adj_cols) are all different. `tile_count`: tiles at positions at or beyond the count are absent. On some devices every slot holds 80 live tiles; on the others slots hold at most half of that.
All inputs are finite; a program needn't handle non-finite values.
Results may differ from the reference program's by a relative error of at most 0.025.
Values may be sent and summed in bfloat16 or wider, within the bound.
No kernel may reach another device: no remote copies, remote signals or barrier semaphores. Data moves between devices by JAX's collectives and lax.ppermute only.
A program may use at most 128 MiB of HBM per device.

```python
import jax
import jax.numpy as jnp
from jax import lax

TILE = 128
F_IN = 128
HID = 256
BLK_DEV = 16
DEG = 5
PER = 80
STEPS = 8
ROWS_DEV = 2048
NODES = 65536
N_BLK = 32
N_REP = 4


def tile_cells(key):
    key_list = jax.random.split(key, N_BLK * N_REP * STEPS)
    cells = jax.vmap(lambda sub_key: jax.random.permutation(sub_key, BLK_DEV * BLK_DEV)[:PER])(key_list)
    return cells.reshape(N_BLK, N_REP, STEPS, PER).astype(jnp.int32)


def draw_adj_rows(key, part):
    cells = tile_cells(key)
    return (cells // BLK_DEV).astype(jnp.int32)


def draw_adj_cols(key, part):
    cells = tile_cells(key)
    return (cells % BLK_DEV).astype(jnp.int32)


def draw_tile_count(key, part):
    key = jax.random.fold_in(key, 7)
    first_key, second_key, third_key = jax.random.split(key, 3)
    base_count = jax.random.randint(first_key, (N_BLK, N_REP, STEPS), max(1, PER // 4), PER // 2 + 1)
    heavy_rows = jax.random.randint(second_key, (N_BLK, N_REP, 1), 0, 8) == 0
    chosen = jax.random.randint(third_key, (), 0, N_BLK * N_REP)
    device = jnp.arange(N_BLK * N_REP, dtype=jnp.int32).reshape(N_BLK, N_REP, 1)
    full_rows = heavy_rows | (device == chosen)
    return jnp.where(full_rows, PER, base_count).astype(jnp.int32)


def steps_of(stream_key, shape, cuts, smallest, largest):
    def one(position, shards_of):
        heights = jax.random.uniform(jax.random.fold_in(jax.random.fold_in(stream_key, 6), position), (shards_of,), jnp.float32, smallest / len(cuts), largest / len(cuts))
        return jnp.repeat(jnp.exp(heights), shape[position] // shards_of).reshape((-1,) + (1,) * (len(shape) - position - 1))

    gain = one(*cuts[0])
    for cut in cuts[1:]:
        gain = gain * one(*cut)
    return gain


def normal_values(rng, extent, width, reach, pieces=(), kind=jnp.bfloat16):
    drawn = jax.random.normal(rng, extent, jnp.float32) * width
    if len(pieces) > 0:
        drawn = steps_of(rng, extent, pieces, -0.22, 0.18) * drawn
    return jnp.clip(drawn, min=-reach, max=reach).astype(kind)


def setup_inputs(seed: int = 0) -> dict:
    seeds = jax.random.split(jax.random.key(seed), 9)
    return {
        "features": normal_values(seeds[0], (NODES, F_IN), 1.0, 6.0, ((0, 32),)),
        "node_order": jax.vmap(lambda own: jax.random.permutation(own, ROWS_DEV))(jax.random.split(seeds[1], N_BLK)).reshape((N_BLK, ROWS_DEV)).astype(jnp.int32),
        "adj_values": normal_values(seeds[2], (N_BLK, N_REP, STEPS, PER, TILE, TILE), (N_BLK * DEG * TILE // 2) ** -0.5, 0.0625, ((0, 32), (1, 4))),
        "adj_rows": draw_adj_rows(jax.random.fold_in(seeds[8], 71), 0),
        "adj_cols": draw_adj_cols(jax.random.fold_in(seeds[8], 71), 0),
        "tile_count": draw_tile_count(jax.random.fold_in(seeds[8], 71), 0),
        "weight": normal_values(seeds[6], (F_IN, HID), F_IN ** -0.5, 0.5),
        "upstream": normal_values(seeds[7], (NODES, HID), 1.0, 6.0, ((0, 128),)),
    }


def placement_matrix(row_index, count, block_count, per_slot):
    levels = jnp.arange(block_count, dtype=jnp.int32)
    live_mask = jnp.arange(per_slot, dtype=jnp.int32) < count
    return ((row_index[None, :] == levels[:, None]) & live_mask[None, :]).astype(jnp.float32)


def reference(features, node_order, adj_values, adj_rows, adj_cols, tile_count, weight, upstream):
    highest = lax.Precision.HIGHEST
    slice_view = features.reshape(N_BLK, ROWS_DEV, F_IN)
    blocked = jax.vmap(lambda rows_in, node_perm: jnp.take(rows_in, node_perm, axis=0))(slice_view, node_order)
    feature_blocks = blocked.reshape(N_BLK, BLK_DEV, TILE, F_IN)

    def forward_slice(slice_id):
        replica_sums = []
        for replica in range(N_REP):
            summed = jnp.zeros((BLK_DEV, TILE, F_IN), jnp.float32)
            for slot_index in range(STEPS):
                column_slice = (slice_id + replica + N_REP * slot_index) % N_BLK
                source = lax.dynamic_index_in_dim(feature_blocks, column_slice, 0, keepdims=False)
                picked = jnp.take(source, adj_cols[slice_id, replica, slot_index], axis=0).astype(jnp.float32)
                tile_values = adj_values[slice_id, replica, slot_index].astype(jnp.float32)
                product = jnp.einsum("ptk,pkf->ptf", tile_values, picked, precision=highest)
                spread_rows = placement_matrix(adj_rows[slice_id, replica, slot_index], tile_count[slice_id, replica, slot_index], BLK_DEV, PER)
                summed = summed + jnp.einsum("bp,ptf->btf", spread_rows, product, precision=highest)
            replica_sums.append(summed)
        return jnp.stack(replica_sums)

    partials = lax.map(forward_slice, jnp.arange(N_BLK, dtype=jnp.int32))
    rounded = lax.optimization_barrier(partials.astype(jnp.bfloat16))
    aggregated = jnp.sum(rounded.astype(jnp.float32), axis=1).astype(jnp.bfloat16).reshape(NODES, F_IN)
    pre_sum = jnp.dot(aggregated, weight, preferred_element_type=jnp.float32)
    sigmoid_gate = jax.nn.sigmoid(pre_sum)
    activations = (pre_sum * sigmoid_gate).astype(jnp.bfloat16)
    grad_pre = (upstream.astype(jnp.float32) * sigmoid_gate * (1.0 + pre_sum * (1.0 - sigmoid_gate))).astype(jnp.bfloat16)
    grad_weight = jnp.dot(aggregated.T, grad_pre, preferred_element_type=jnp.float32)
    back_proj = jnp.dot(grad_pre, weight.T, preferred_element_type=jnp.float32).astype(jnp.bfloat16)
    back_blocks = back_proj.reshape(N_BLK, BLK_DEV, TILE, F_IN)

    def backward_slice(grads, slice_id):
        own_rows = lax.dynamic_index_in_dim(back_blocks, slice_id, 0, keepdims=False)
        for replica in range(N_REP):
            for slot_index in range(STEPS):
                column_slice = (slice_id + replica + N_REP * slot_index) % N_BLK
                picked = jnp.take(own_rows, adj_rows[slice_id, replica, slot_index], axis=0).astype(jnp.float32)
                tile_values = adj_values[slice_id, replica, slot_index].astype(jnp.float32)
                product = jnp.einsum("ptk,ptf->pkf", tile_values, picked, precision=highest)
                spread_cols = placement_matrix(adj_cols[slice_id, replica, slot_index], tile_count[slice_id, replica, slot_index], BLK_DEV, PER)
                contrib = jnp.einsum("bp,pkf->bkf", spread_cols, product, precision=highest)
                grads = grads.at[replica, column_slice].add(contrib)
        return grads, None

    grads = lax.scan(backward_slice, jnp.zeros((N_REP, N_BLK, BLK_DEV, TILE, F_IN), jnp.float32), jnp.arange(N_BLK, dtype=jnp.int32))[0]
    rounded_grads = lax.optimization_barrier(grads.astype(jnp.bfloat16))
    grad_blocked = jnp.sum(rounded_grads.astype(jnp.float32), axis=0).reshape(N_BLK, ROWS_DEV, F_IN)
    restored = jax.vmap(lambda rows_in, node_perm: jnp.zeros_like(rows_in).at[node_perm].set(rows_in))(grad_blocked, node_order)
    grad_features = restored.reshape(NODES, F_IN).astype(jnp.bfloat16)
    return activations, grad_weight, grad_features
```

```python
import functools

import jax
import jax.numpy as jnp
import numpy as np
from jax import lax
from jax.experimental import pallas as pl
from jax.experimental.pallas import tpu as pltpu
from jax.sharding import PartitionSpec as P

TILE = 128
FORWARD_TURN = 4
BACKWARD_TURN = 8
FORWARD_WIDTH = 8
BACKWARD_WIDTH = 4
FORWARD_WAVES = ((0, 1, 3, 2), (4, 5, 7, 6))
BACKWARD_WAVES = ((4, 5, 6, 7), (0, 1, 2, 3))
PAIR = 2
CODE = 256
VMEM_LIMIT = 12 * 1024 * 1024
HOLD_LIMIT = 32 * 1024 * 1024


def spots():
    return [(x, y, z, c) for x in range(4) for y in range(4) for z in range(4) for c in range(2)]


def coords(x, y, z, c):
    return 8 * y + 2 * z + x % 2, x // 2 * 2 + c


def device(x, y, z, c):
    blk, rep = coords(x % 4, y % 4, z % 4, c)
    return 4 * blk + rep


def levels(x, y, z, c):
    kind = sum(coords(x, y, z, c)) % 4
    level = z if kind // 2 == z % 2 else z + 1
    return kind % 2, (level + 2 * c) % 4, (level + 2 - 2 * c) % 4


def slot_table():
    table = np.zeros((128, 8), np.int32)
    for spot in spots():
        low, near, far = levels(*spot)
        base = sum(coords(*spot))
        for item in range(8):
            row = (spot[1] + item) % 4
            wanted = 8 * row + 2 * (near if item < 4 else far) + low
            table[device(*spot), item] = (wanted - base) % 32 // 4
    return table


def fetch_pairs():
    listed = []
    for x, y, z, c in spots():
        near = levels(x, y, z, c)[1]
        listed.append((device(x - c, y, near, c), device(x, y, z, c)))
    return listed


def partner_pairs():
    return [(device(x, y, z, c), device(x + 2 * c - 1, y, z, 1 - c)) for x, y, z, c in spots()]


def blk_steps():
    near, across = (1, 0, 3, 2), (3, 2, 1, 0)
    return [
        [(device(x, y, z, c), device(x, ring[y], z, c)) for x, y, z, c in spots()]
        for ring in (near, across)
    ] + [
        [(device(x, y, z, c), device(x, y, ring[z], c)) for x, y, z, c in spots()]
        for ring in (near, across)
    ] + [
        [(device(x, y, z, c), device(near[x], y, z, c)) for x, y, z, c in spots()]
    ]


def ring_pairs(step):
    return [(device(x, y, z, c), device(x, y + step, z, c)) for x, y, z, c in spots()]


def params(limit=VMEM_LIMIT):
    return pltpu.CompilerParams(vmem_limit_bytes=limit)


def whole():
    return pl.BlockSpec(memory_space=pltpu.VMEM)


def order_kernel(order_ref, feat_ref, out_ref):
    rows = feat_ref.shape[0]
    step = 512
    feats = feat_ref[...]
    for start in range(0, rows, step):
        parts = []
        for inner in range(start, start + step, TILE):
            line = order_ref[0:1, inner : inner + TILE]
            parts.append(jnp.broadcast_to(line, (TILE, TILE)).T)
        column = jnp.concatenate(parts, axis=0)
        pieces = []
        for col in range(0, rows, TILE):
            level = lax.broadcasted_iota(jnp.int32, (step, TILE), 1) + col
            pieces.append((column == level).astype(jnp.float32).astype(jnp.bfloat16))
        pick = jnp.concatenate(pieces, axis=1)
        out_ref[start : start + step, :] = jnp.dot(
            pick, feats, preferred_element_type=jnp.float32
        ).astype(jnp.bfloat16)


def order_rows(order, features):
    return pl.pallas_call(
        order_kernel,
        out_shape=jax.ShapeDtypeStruct(features.shape, jnp.bfloat16),
        in_specs=[whole(), whole()],
        out_specs=whole(),
        compiler_params=params(),
    )(order, features)


def hold_kernel(items, place_ref, tiles_ref, out_ref, sems):
    per_slot = out_ref.shape[0] // len(items)
    copies = []
    for number, item in enumerate(items):
        copies.append(
            pltpu.make_async_copy(
                tiles_ref.at[pl.ds(place_ref[1 + item] * per_slot, per_slot)],
                out_ref.at[pl.ds(number * per_slot, per_slot)],
                sems.at[number],
            )
        )
        copies[-1].start()
    for copy in copies:
        copy.wait()


def hold(items, place, tiles, per_slot):
    size = len(items) * per_slot
    return pl.pallas_call(
        functools.partial(hold_kernel, items),
        out_shape=jax.ShapeDtypeStruct((size, TILE, TILE), tiles.dtype),
        grid_spec=pltpu.PrefetchScalarGridSpec(
            num_scalar_prefetch=1,
            grid=(),
            in_specs=[pl.BlockSpec(memory_space=pltpu.HBM)],
            out_specs=whole(),
            scratch_shapes=[pltpu.SemaphoreType.DMA((len(items),))],
        ),
        compiler_params=params(HOLD_LIMIT),
        cost_estimate=pl.CostEstimate(
            flops=0, bytes_accessed=4 * size * TILE * TILE, transcendentals=0
        ),
    )(place, tiles)


def tile_lists(key, source, target_count, zero, width, turn):
    lists, size = key.shape
    capacity = (size + target_count * (width - 1)) // width
    capacity = -(-capacity // turn) * turn
    ids = jnp.arange(size, dtype=jnp.int32)
    levels = jnp.arange(target_count, dtype=jnp.int32)
    earlier = (key[:, None, :] == key[:, :, None]) & (ids[None, :] < ids[:, None])
    rank = jnp.sum(earlier.astype(jnp.int32), axis=2)
    held = jnp.sum((key[:, None, :] == levels[:, None]).astype(jnp.int32), axis=2)
    needed = (held + width - 1) // width
    upto = levels[None, :] <= levels[:, None]
    ends = jnp.sum(jnp.where(upto, needed[:, None, :], 0), axis=2)
    base = jnp.sum(jnp.where(levels < key[:, :, None], needed[:, None, :], 0), axis=2)
    place = jnp.where(key < target_count, base * width + rank, -1)
    cells = jnp.arange(capacity * width, dtype=jnp.int32)
    hit = (place[:, None, :] == cells[:, None]).astype(jnp.int32)
    tile = jnp.sum(hit * ids, axis=2)
    origin = zero + jnp.sum(hit * (source - zero)[:, None, :], axis=2)
    groups = jnp.arange(capacity, dtype=jnp.int32)
    target = jnp.sum((ends[:, None, :] <= groups[:, None]).astype(jnp.int32), axis=2)
    code = tile * CODE + origin
    packed = jnp.concatenate([code.reshape(-1), target.reshape(-1), jnp.max(ends, axis=1)])
    return packed, capacity


def group_turns(groups, length, target_of, store, product):
    def turn(index, total):
        for lane in range(length):
            group = index * length + lane
            target = target_of(group)
            new = (group == 0) | (target != target_of(jnp.maximum(group - 1, 0)))
            fresh = product(group)
            total = jnp.where(new, fresh, total + fresh)
            store(pl.ds(pl.multiple_of(target * TILE, TILE), TILE), total)
        return total

    turns = (groups + length - 1) // length
    lax.fori_loop(0, turns, turn, jnp.zeros((TILE, TILE), jnp.float32))


def forward_kernel(pieces, lists, wave, capacity, list_ref, hold_ref, *refs):
    first = wave == 0
    x_refs, refs = refs[:pieces], refs[pieces:]
    if first:
        total_ref, x_ref = refs
        total_ref[...] = jnp.zeros_like(total_ref)
    else:
        before_ref, out_refs, (total_ref, x_ref) = refs[0], refs[1:-2], refs[-2:]
        total_ref[...] = before_ref[...].astype(jnp.bfloat16)
    start = 0
    for piece_ref in x_refs:
        x_ref[start : start + piece_ref.shape[0], :] = piece_ref[...]
        start += piece_ref.shape[0]
    x_ref[start:, :] = jnp.zeros((TILE, TILE), jnp.bfloat16)

    def product(group):
        begin = (wave * capacity + group) * FORWARD_WIDTH
        codes = [list_ref[begin + item] for item in range(FORWARD_WIDTH)]
        left = jnp.concatenate([hold_ref[code // CODE] for code in codes], axis=1)
        starts = [pl.multiple_of(code % CODE * TILE, TILE) for code in codes]
        right = jnp.concatenate([x_ref[pl.ds(start, TILE), :] for start in starts], axis=0)
        return jnp.dot(left, right, preferred_element_type=jnp.float32)

    def store(span, total):
        if first:
            total_ref[span, :] = total
        else:
            total_ref[span, :] = (total + before_ref[span, :]).astype(jnp.bfloat16)

    codes = lists * capacity * FORWARD_WIDTH
    ends = codes + lists * capacity
    group_turns(
        list_ref[ends + wave],
        FORWARD_TURN,
        lambda group: list_ref[codes + wave * capacity + group],
        store,
        product,
    )
    if not first:
        reps = len(out_refs)
        own = out_refs[0].shape[0]
        here = list_ref[ends + lists]
        for shift, out_ref in enumerate(out_refs):
            start = pl.multiple_of((here + shift) % reps * own, own)
            out_ref[...] = total_ref[pl.ds(start, own), :]


def estimate(tiles):
    return pl.CostEstimate(
        flops=8 * tiles * TILE**3, bytes_accessed=tiles * TILE * TILE * 2, transcendentals=0
    )


def forward_product(rows, lists, wave, packed, capacity, held, xs, before, reps):
    first = wave == 0
    total_shape = (rows + TILE, TILE)
    x_rows = sum(x.shape[0] for x in xs)
    x_scratch = pltpu.VMEM((x_rows + TILE, TILE), jnp.bfloat16)
    if first:
        operands = [held, *xs]
        out_shape = jax.ShapeDtypeStruct(total_shape, jnp.float32)
        out_specs = whole()
        scratch = [x_scratch]
    else:
        operands = [held, *xs, before]
        out_shape = [jax.ShapeDtypeStruct((rows // reps, TILE), jnp.bfloat16)] * reps
        out_specs = [whole()] * reps
        scratch = [pltpu.VMEM(total_shape, jnp.bfloat16), x_scratch]
    return pl.pallas_call(
        functools.partial(forward_kernel, len(xs), lists, wave, capacity),
        out_shape=out_shape,
        grid_spec=pltpu.PrefetchScalarGridSpec(
            num_scalar_prefetch=1,
            grid=(),
            in_specs=[whole()] * len(operands),
            out_specs=out_specs,
            scratch_shapes=scratch,
        ),
        compiler_params=params(),
        cost_estimate=estimate(held.shape[0]),
    )(packed, *operands)


def dense_kernel(*refs):
    part_refs, (weight_ref, upstream_ref, act_ref, pay_ref) = refs[:-4], refs[-4:]
    rows = upstream_ref.shape[0]
    total = part_refs[0][...].astype(jnp.float32)
    for part_ref in part_refs[1:]:
        total = total + part_ref[...].astype(jnp.float32)
    aggregated = total.astype(jnp.bfloat16)
    weight = weight_ref[...]
    pre = jnp.dot(aggregated, weight, preferred_element_type=jnp.float32)
    gate = jax.nn.sigmoid(pre)
    act_ref[...] = (pre * gate).astype(jnp.bfloat16)
    grad_pre = (
        upstream_ref[...].astype(jnp.float32) * gate * (1.0 + pre * (1.0 - gate))
    ).astype(jnp.bfloat16)
    back = lax.dot_general(
        weight, grad_pre, (((1,), (1,)), ((), ())), preferred_element_type=jnp.float32
    ).astype(jnp.bfloat16)
    for block in range(rows // TILE):
        pay_ref[block * TILE : (block + 1) * TILE, :] = back[:, block * TILE : (block + 1) * TILE]
    local = lax.dot_general(
        aggregated, grad_pre, (((0,), (0,)), ((), ())), preferred_element_type=jnp.float32
    ).astype(jnp.bfloat16)
    for half in range(weight.shape[1] // TILE):
        pay_ref[rows + half * TILE : rows + (half + 1) * TILE, :] = local[
            :, half * TILE : (half + 1) * TILE
        ]


def dense_layer(parts, weight, upstream):
    rows, hidden = upstream.shape
    pay_rows = rows + hidden // TILE * weight.shape[0]
    return pl.pallas_call(
        dense_kernel,
        out_shape=(
            jax.ShapeDtypeStruct((rows, hidden), jnp.bfloat16),
            jax.ShapeDtypeStruct((pay_rows, TILE), jnp.bfloat16),
        ),
        in_specs=[whole()] * (len(parts) + 2),
        out_specs=(whole(), whole()),
        compiler_params=params(),
    )(*parts, weight, upstream)


def backward_kernel(count, lists, first, capacity, list_ref, hold_ref, *refs):
    pay_refs, out_refs = refs[: -2 - count], refs[-2 - count : -2]
    total_ref, back_ref = refs[-2:]
    reps = len(pay_refs)
    rows = out_refs[0].shape[0]
    own = rows // reps
    per_slot = hold_ref.shape[0] // count
    codes = lists * capacity * BACKWARD_WIDTH
    ends = codes + lists * capacity
    place = ends + lists
    here = list_ref[place]
    for shift, pay_ref in enumerate(pay_refs):
        start = pl.multiple_of((here + reps - shift) % reps * own, own)
        back_ref[pl.ds(start, own), :] = pay_ref[:own, :]
    back_ref[rows:, :] = jnp.zeros((TILE, TILE), jnp.bfloat16)
    total_ref[...] = jnp.zeros_like(total_ref)
    for number in range(0, count, PAIR):
        listed = first + number // PAIR

        def product(group, listed=listed, number=number):
            begin = (listed * capacity + group) * BACKWARD_WIDTH
            items = [list_ref[begin + item] for item in range(BACKWARD_WIDTH)]
            starts = [pl.multiple_of(code % CODE * TILE, TILE) for code in items]
            left = jnp.concatenate([back_ref[pl.ds(start, TILE), :] for start in starts], axis=1)
            right = jnp.concatenate(
                [hold_ref[number * per_slot + code // CODE] for code in items], axis=0
            )
            return jnp.dot(left, right, preferred_element_type=jnp.float32)

        def target_of(group, listed=listed):
            return list_ref[codes + listed * capacity + group]

        def store(span, total):
            total_ref[span, :] = total.astype(jnp.bfloat16)

        group_turns(list_ref[ends + listed], BACKWARD_TURN, target_of, store, product)
        for item in range(PAIR):
            out_refs[number + item][...] = total_ref[item * rows : (item + 1) * rows, :]
        if number + PAIR < count:
            total_ref[...] = jnp.zeros_like(total_ref)


def backward_product(count, rows, lists, first, packed, capacity, held, pays):
    out_shape = jax.ShapeDtypeStruct((rows, TILE), jnp.bfloat16)
    return pl.pallas_call(
        functools.partial(backward_kernel, count, lists, first, capacity),
        out_shape=[out_shape] * count,
        grid_spec=pltpu.PrefetchScalarGridSpec(
            num_scalar_prefetch=1,
            grid=(),
            in_specs=[whole()] * (1 + len(pays)),
            out_specs=[whole()] * count,
            scratch_shapes=[
                pltpu.VMEM((PAIR * rows + TILE, TILE), jnp.bfloat16),
                pltpu.VMEM((rows + TILE, TILE), jnp.bfloat16),
            ],
        ),
        compiler_params=params(),
        cost_estimate=estimate(held.shape[0]),
    )(packed, held, *pays)


def restore_kernel(place_ref, order_ref, home_ref, *refs):
    out_refs, part_ref = refs[:-1], refs[-1]
    rows = order_ref.shape[1]
    reps = len(out_refs)
    own = rows // reps
    for block in range(rows // TILE):
        span = slice(block * TILE, (block + 1) * TILE)
        part_ref[span, :] = home_ref[span, :].astype(jnp.float32).T.astype(jnp.bfloat16)
    order = order_ref[...]
    part = part_ref[...]
    for shift, out_ref in enumerate(out_refs):
        start = (place_ref[0] + shift) % reps * own
        level = lax.broadcasted_iota(jnp.int32, (own, rows), 0) + start
        pick = (jnp.broadcast_to(order, (own, rows)) == level).astype(jnp.float32)
        out_ref[...] = jnp.dot(
            pick.astype(jnp.bfloat16), part, preferred_element_type=jnp.float32
        ).astype(jnp.bfloat16)


def restore(place, order, home, reps):
    rows = order.shape[1]
    out_shape = jax.ShapeDtypeStruct((rows // reps, TILE), jnp.bfloat16)
    return pl.pallas_call(
        restore_kernel,
        out_shape=[out_shape] * reps,
        grid_spec=pltpu.PrefetchScalarGridSpec(
            num_scalar_prefetch=1,
            grid=(),
            in_specs=[whole()] * 2,
            out_specs=[whole()] * reps,
            scratch_shapes=[pltpu.VMEM((rows, TILE), jnp.bfloat16)],
        ),
        compiler_params=params(),
    )(place, order, home)


def added(*values):
    return sum(value.astype(jnp.float32) for value in values).astype(jnp.bfloat16)


def per_device(features, node_order, adj_values, adj_rows, adj_cols, tile_count, weight, upstream):
    reps = lax.axis_size("rep")
    slices = lax.axis_size("blk")
    steps = slices // reps
    rows_dev = features.shape[0]
    blocks = rows_dev // TILE
    both = ("blk", "rep")
    row_ids, col_ids, counts = adj_rows[0, 0], adj_cols[0, 0], tile_count[0, 0]
    per_slot = row_ids.shape[1]
    tiles = adj_values.reshape((-1, TILE, TILE))
    own_rep = lax.axis_index("rep").astype(jnp.int32).reshape(1)

    here = lax.axis_index("blk") * reps + lax.axis_index("rep")
    slots = lax.dynamic_index_in_dim(jnp.asarray(slot_table()), here, 0, keepdims=False)
    place = jnp.concatenate([own_rep, slots])
    half = rows_dev // 2

    def moved(value, listed):
        return lax.ppermute(value, both, listed)

    def up(value):
        return moved(value, ring_pairs(1))

    def down(value):
        return moved(value, ring_pairs(-1))

    def swapped(value):
        return moved(value, partner_pairs())

    def to_reps(values):
        received = [values[0]]
        for shift in range(1, reps):
            along = [(rep, (rep + shift) % reps) for rep in range(reps)]
            received.append(lax.ppermute(values[shift], "rep", along))
        return received

    blocked = order_rows(node_order, features)
    near = moved(blocked, fetch_pairs())
    above, below = down(near), up(near)
    far = swapped(near)
    above, far = lax.optimization_barrier((above, far))
    middle = [down(above[:half]), up(below[half:])]
    arrived = {0: [near], 1: [above], 2: middle, 3: [below], 4: [far], 5: [swapped(above)]}
    arrived[6] = [swapped(value) for value in middle]
    arrived[7] = [swapped(below)]
    alive = jnp.arange(per_slot, dtype=jnp.int32)[None, :] < counts[:, None]
    cells = jnp.take(jnp.where(alive, row_ids * CODE + col_ids, -1), slots, axis=0)

    def split(cells, items):
        chosen = jnp.concatenate([cells[item : item + 1] for item in items])
        return chosen >= 0, chosen // CODE, chosen % CODE

    waves = len(FORWARD_WAVES)
    alive, rows_of, cols_of = split(cells, sum(FORWARD_WAVES, ()))
    offsets = jnp.arange(steps, dtype=jnp.int32)[:, None] % (steps // waves) * blocks
    packed, capacity = tile_lists(
        jnp.where(alive, rows_of, blocks).reshape(waves, -1),
        (cols_of + offsets).reshape(waves, -1),
        blocks,
        steps // waves * blocks,
        FORWARD_WIDTH,
        FORWARD_TURN,
    )
    packed = jnp.concatenate([packed, own_rep])
    places = []
    for item in (0, 1):
        known, arrived[item][0] = lax.optimization_barrier((place, arrived[item][0]))
        places.append(known)
    total = None
    for wave, items in enumerate(FORWARD_WAVES):
        xs = sum([arrived[item] for item in items], [])
        held = hold(items, places[wave], tiles, per_slot)
        total = forward_product(
            rows_dev, waves, wave, packed, capacity, held, xs, total, reps
        )
    total = list(total)
    last_cells, total[0] = lax.optimization_barrier((cells, total[0]))
    shared = to_reps(total)
    lists = steps // PAIR
    alive, rows_of, cols_of = split(last_cells, sum(BACKWARD_WAVES, ()))
    offsets = jnp.arange(steps, dtype=jnp.int32)[:, None] % PAIR * blocks
    packed, capacity = tile_lists(
        jnp.where(alive, cols_of + offsets, PAIR * blocks).reshape(lists, -1),
        rows_of.reshape(lists, -1),
        PAIR * blocks,
        blocks,
        BACKWARD_WIDTH,
        BACKWARD_TURN,
    )
    packed = jnp.concatenate([packed, own_rep])
    shared[1], packed = lax.optimization_barrier((shared[1], packed))
    activations, pay = dense_layer(shared, weight, upstream)
    late_place, pay = lax.optimization_barrier((place, pay))
    pays = to_reps([pay] * reps)
    holds = [hold(items, late_place, tiles, per_slot) for items in BACKWARD_WAVES]
    packed, holds = lax.optimization_barrier((packed, holds))

    def products(wave, packed):
        count = len(BACKWARD_WAVES[wave])
        first = wave * count // PAIR
        return list(
            backward_product(count, rows_dev, lists, first, packed, capacity, holds[wave], pays)
        )

    grad_weight = sum(pay[-weight.size // TILE :].astype(jnp.float32) for pay in pays)
    todo = blk_steps()

    def next_after(total, value):
        total, value = lax.optimization_barrier((total, value))
        return total + moved(total, todo.pop(0)), value

    step = moved(grad_weight, todo.pop(0))
    others = products(0, packed)
    step, packed, others[0] = lax.optimization_barrier((step, packed, others[0]))
    grad_weight = grad_weight + step
    returned = {item: swapped(others[item]) for item in (2, 1, 3, 0)}
    mine = products(1, packed)
    two = added(mine[2], returned[2])
    from_below, from_above = up(two[:half]), down(two[half:])
    grad_weight, returned[1] = next_after(grad_weight, returned[1])
    one = jnp.concatenate(
        [added(mine[1][:half], returned[1][:half], from_below), added(mine[1][half:], returned[1][half:])]
    )
    three = jnp.concatenate(
        [added(mine[3][:half], returned[3][:half]), added(mine[3][half:], returned[3][half:], from_above)]
    )
    onward = [up(one), down(three)]
    grad_weight, returned[0] = next_after(grad_weight, returned[0])
    ended = added(mine[0], returned[0], *onward)
    grad_weight, ended = next_after(grad_weight, ended)
    home = moved(ended, [(user, owner) for owner, user in fetch_pairs()])
    grad_weight, home = next_after(grad_weight, home)
    terms = to_reps(restore(own_rep, node_order, home, reps))
    grad_features = added(*terms)
    stacked = grad_weight.reshape(weight.shape[1] // TILE, weight.shape[0], TILE)
    grad_weight = jnp.concatenate([stacked[half] for half in range(stacked.shape[0])], axis=1)
    return (activations, grad_weight, grad_features)


def solution(mesh):
    placed = (
        P("blk", None),
        P("blk", None),
        P("blk", "rep", None, None, None, None),
        P("blk", "rep", None, None),
        P("blk", "rep", None, None),
        P("blk", "rep", None),
        P(),
        P(("blk", "rep"), None),
    )
    return jax.shard_map(
        per_device,
        mesh=mesh,
        in_specs=placed,
        out_specs=(P(("blk", "rep"), None), P(), P(("blk", "rep"), None)),
        check_vma=False,
    )
```

```python
import functools

import jax
import jax.numpy as jnp
import numpy as np
from jax import lax
from jax.experimental import pallas as pl
from jax.experimental.pallas import tpu as pltpu
from jax.sharding import PartitionSpec as P

TILE = 128
FORWARD_TURN = 4
BACKWARD_TURN = 8
FORWARD_WIDTH = 8
BACKWARD_WIDTH = 4
FORWARD_WAVES = ((0, 1, 3, 2), (4, 5, 7, 6))
BACKWARD_WAVES = ((4, 5, 6, 7), (0, 1, 2, 3))
PAIR = 2
PARTS = 4
CODE = 256
VMEM_LIMIT = 12 * 1024 * 1024
HOLD_LIMIT = 32 * 1024 * 1024


def spots():
    return [(x, y, z, c) for x in range(4) for y in range(4) for z in range(4) for c in range(2)]


def coords(x, y, z, c):
    return 8 * y + 2 * z + x % 2, x // 2 * 2 + c


def device(x, y, z, c):
    blk, rep = coords(x % 4, y % 4, z % 4, c)
    return 4 * blk + rep


def levels(x, y, z, c):
    kind = sum(coords(x, y, z, c)) % 4
    level = z if kind // 2 == z % 2 else z + 1
    return kind % 2, (level + 2 * c) % 4, (level + 2 - 2 * c) % 4


def slot_table():
    table = np.zeros((128, 8), np.int32)
    for spot in spots():
        low, near, far = levels(*spot)
        base = sum(coords(*spot))
        for item in range(8):
            row = (spot[1] + item) % 4
            wanted = 8 * row + 2 * (near if item < 4 else far) + low
            table[device(*spot), item] = (wanted - base) % 32 // 4
    return table


def fetch_pairs():
    listed = []
    for x, y, z, c in spots():
        near = levels(x, y, z, c)[1]
        listed.append((device(x - c, y, near, c), device(x, y, z, c)))
    return listed


def partner_pairs():
    return [(device(x, y, z, c), device(x + 2 * c - 1, y, z, 1 - c)) for x, y, z, c in spots()]


def blk_steps():
    near, across = (1, 0, 3, 2), (3, 2, 1, 0)
    return [
        [(device(x, y, z, c), device(x, ring[y], z, c)) for x, y, z, c in spots()]
        for ring in (near, across)
    ] + [
        [(device(x, y, z, c), device(x, y, ring[z], c)) for x, y, z, c in spots()]
        for ring in (near, across)
    ] + [
        [(device(x, y, z, c), device(near[x], y, z, c)) for x, y, z, c in spots()]
    ]


def ring_pairs(step):
    return [(device(x, y, z, c), device(x, y + step, z, c)) for x, y, z, c in spots()]


def params(limit=VMEM_LIMIT):
    return pltpu.CompilerParams(vmem_limit_bytes=limit)


def whole():
    return pl.BlockSpec(memory_space=pltpu.VMEM)


def order_kernel(order_ref, feat_ref, out_ref):
    rows = feat_ref.shape[0]
    step = 512
    feats = feat_ref[...]
    for start in range(0, rows, step):
        parts = []
        for inner in range(start, start + step, TILE):
            line = order_ref[0:1, inner : inner + TILE]
            parts.append(jnp.broadcast_to(line, (TILE, TILE)).T)
        column = jnp.concatenate(parts, axis=0)
        pieces = []
        for col in range(0, rows, TILE):
            level = lax.broadcasted_iota(jnp.int32, (step, TILE), 1) + col
            pieces.append((column == level).astype(jnp.float32).astype(jnp.bfloat16))
        pick = jnp.concatenate(pieces, axis=1)
        out_ref[start : start + step, :] = jnp.dot(
            pick, feats, preferred_element_type=jnp.float32
        ).astype(jnp.bfloat16)


def order_rows(order, features):
    return pl.pallas_call(
        order_kernel,
        out_shape=jax.ShapeDtypeStruct(features.shape, jnp.bfloat16),
        in_specs=[whole(), whole()],
        out_specs=whole(),
        compiler_params=params(),
    )(order, features)


def hold_kernel(items, place_ref, tiles_ref, out_ref, sems):
    per_slot = out_ref.shape[0] // len(items)
    part = per_slot // PARTS
    copies = []
    for number, item in enumerate(items):
        for piece in range(PARTS):
            source = place_ref[1 + item] * per_slot + piece * part
            target = number * per_slot + piece * part
            copies.append(
                pltpu.make_async_copy(
                    tiles_ref.at[pl.ds(source, part)],
                    out_ref.at[pl.ds(target, part)],
                    sems.at[number * PARTS + piece],
                )
            )
            copies[-1].start()
    for copy in copies:
        copy.wait()


def hold(items, place, tiles, per_slot):
    size = len(items) * per_slot
    return pl.pallas_call(
        functools.partial(hold_kernel, items),
        out_shape=jax.ShapeDtypeStruct((size, TILE, TILE), tiles.dtype),
        grid_spec=pltpu.PrefetchScalarGridSpec(
            num_scalar_prefetch=1,
            grid=(),
            in_specs=[pl.BlockSpec(memory_space=pltpu.HBM)],
            out_specs=whole(),
            scratch_shapes=[pltpu.SemaphoreType.DMA((len(items) * PARTS,))],
        ),
        compiler_params=params(HOLD_LIMIT),
        cost_estimate=pl.CostEstimate(
            flops=0, bytes_accessed=4 * size * TILE * TILE, transcendentals=0
        ),
    )(place, tiles)


def tile_lists(key, source, target_count, zero, width, turn):
    lists, size = key.shape
    capacity = (size + target_count * (width - 1)) // width
    capacity = -(-capacity // turn) * turn
    ids = jnp.arange(size, dtype=jnp.int32)
    levels = jnp.arange(target_count, dtype=jnp.int32)
    earlier = (key[:, None, :] == key[:, :, None]) & (ids[None, :] < ids[:, None])
    rank = jnp.sum(earlier.astype(jnp.int32), axis=2)
    held = jnp.sum((key[:, None, :] == levels[:, None]).astype(jnp.int32), axis=2)
    needed = (held + width - 1) // width
    upto = levels[None, :] <= levels[:, None]
    ends = jnp.sum(jnp.where(upto, needed[:, None, :], 0), axis=2)
    base = jnp.sum(jnp.where(levels < key[:, :, None], needed[:, None, :], 0), axis=2)
    place = jnp.where(key < target_count, base * width + rank, -1)
    cells = jnp.arange(capacity * width, dtype=jnp.int32)
    hit = (place[:, None, :] == cells[:, None]).astype(jnp.int32)
    tile = jnp.sum(hit * ids, axis=2)
    origin = zero + jnp.sum(hit * (source - zero)[:, None, :], axis=2)
    groups = jnp.arange(capacity, dtype=jnp.int32)
    target = jnp.sum((ends[:, None, :] <= groups[:, None]).astype(jnp.int32), axis=2)
    code = tile * CODE + origin
    packed = jnp.concatenate([code.reshape(-1), target.reshape(-1), jnp.max(ends, axis=1)])
    return packed, capacity


def group_turns(groups, length, target_of, store, product):
    def turn(index, total):
        for lane in range(length):
            group = index * length + lane
            target = target_of(group)
            new = (group == 0) | (target != target_of(jnp.maximum(group - 1, 0)))
            fresh = product(group)
            total = jnp.where(new, fresh, total + fresh)
            store(pl.ds(pl.multiple_of(target * TILE, TILE), TILE), total)
        return total

    turns = (groups + length - 1) // length
    lax.fori_loop(0, turns, turn, jnp.zeros((TILE, TILE), jnp.float32))


def forward_kernel(pieces, lists, wave, capacity, list_ref, hold_ref, *refs):
    first = wave == 0
    x_refs, refs = refs[:pieces], refs[pieces:]
    if first:
        total_ref, x_ref = refs
        total_ref[...] = jnp.zeros_like(total_ref)
    else:
        before_ref, out_refs, (total_ref, x_ref) = refs[0], refs[1:-2], refs[-2:]
        total_ref[...] = before_ref[...].astype(jnp.bfloat16)
    start = 0
    for piece_ref in x_refs:
        x_ref[start : start + piece_ref.shape[0], :] = piece_ref[...]
        start += piece_ref.shape[0]
    x_ref[start:, :] = jnp.zeros((TILE, TILE), jnp.bfloat16)

    def product(group):
        begin = (wave * capacity + group) * FORWARD_WIDTH
        codes = [list_ref[begin + item] for item in range(FORWARD_WIDTH)]
        left = jnp.concatenate([hold_ref[code // CODE] for code in codes], axis=1)
        starts = [pl.multiple_of(code % CODE * TILE, TILE) for code in codes]
        right = jnp.concatenate([x_ref[pl.ds(start, TILE), :] for start in starts], axis=0)
        return jnp.dot(left, right, preferred_element_type=jnp.float32)

    def store(span, total):
        if first:
            total_ref[span, :] = total
        else:
            total_ref[span, :] = (total + before_ref[span, :]).astype(jnp.bfloat16)

    codes = lists * capacity * FORWARD_WIDTH
    ends = codes + lists * capacity
    group_turns(
        list_ref[ends + wave],
        FORWARD_TURN,
        lambda group: list_ref[codes + wave * capacity + group],
        store,
        product,
    )
    if not first:
        reps = len(out_refs)
        own = out_refs[0].shape[0]
        here = list_ref[ends + lists]
        for shift, out_ref in enumerate(out_refs):
            start = pl.multiple_of((here + shift) % reps * own, own)
            out_ref[...] = total_ref[pl.ds(start, own), :]


def estimate(tiles):
    return pl.CostEstimate(
        flops=8 * tiles * TILE**3, bytes_accessed=tiles * TILE * TILE * 2, transcendentals=0
    )


def forward_product(rows, lists, wave, packed, capacity, held, xs, before, reps):
    first = wave == 0
    total_shape = (rows + TILE, TILE)
    x_rows = sum(x.shape[0] for x in xs)
    x_scratch = pltpu.VMEM((x_rows + TILE, TILE), jnp.bfloat16)
    if first:
        operands = [held, *xs]
        out_shape = jax.ShapeDtypeStruct(total_shape, jnp.float32)
        out_specs = whole()
        scratch = [x_scratch]
    else:
        operands = [held, *xs, before]
        out_shape = [jax.ShapeDtypeStruct((rows // reps, TILE), jnp.bfloat16)] * reps
        out_specs = [whole()] * reps
        scratch = [pltpu.VMEM(total_shape, jnp.bfloat16), x_scratch]
    return pl.pallas_call(
        functools.partial(forward_kernel, len(xs), lists, wave, capacity),
        out_shape=out_shape,
        grid_spec=pltpu.PrefetchScalarGridSpec(
            num_scalar_prefetch=1,
            grid=(),
            in_specs=[whole()] * len(operands),
            out_specs=out_specs,
            scratch_shapes=scratch,
        ),
        compiler_params=params(),
        cost_estimate=estimate(held.shape[0]),
    )(packed, *operands)


def dense_kernel(*refs):
    part_refs, (weight_ref, upstream_ref, act_ref, pay_ref) = refs[:-4], refs[-4:]
    rows = upstream_ref.shape[0]
    total = part_refs[0][...].astype(jnp.float32)
    for part_ref in part_refs[1:]:
        total = total + part_ref[...].astype(jnp.float32)
    aggregated = total.astype(jnp.bfloat16)
    weight = weight_ref[...]
    pre = jnp.dot(aggregated, weight, preferred_element_type=jnp.float32)
    gate = jax.nn.sigmoid(pre)
    act_ref[...] = (pre * gate).astype(jnp.bfloat16)
    grad_pre = (
        upstream_ref[...].astype(jnp.float32) * gate * (1.0 + pre * (1.0 - gate))
    ).astype(jnp.bfloat16)
    back = lax.dot_general(
        weight, grad_pre, (((1,), (1,)), ((), ())), preferred_element_type=jnp.float32
    ).astype(jnp.bfloat16)
    for block in range(rows // TILE):
        pay_ref[block * TILE : (block + 1) * TILE, :] = back[:, block * TILE : (block + 1) * TILE]
    local = lax.dot_general(
        aggregated, grad_pre, (((0,), (0,)), ((), ())), preferred_element_type=jnp.float32
    ).astype(jnp.bfloat16)
    for half in range(weight.shape[1] // TILE):
        pay_ref[rows + half * TILE : rows + (half + 1) * TILE, :] = local[
            :, half * TILE : (half + 1) * TILE
        ]


def dense_layer(parts, weight, upstream):
    rows, hidden = upstream.shape
    pay_rows = rows + hidden // TILE * weight.shape[0]
    return pl.pallas_call(
        dense_kernel,
        out_shape=(
            jax.ShapeDtypeStruct((rows, hidden), jnp.bfloat16),
            jax.ShapeDtypeStruct((pay_rows, TILE), jnp.bfloat16),
        ),
        in_specs=[whole()] * (len(parts) + 2),
        out_specs=(whole(), whole()),
        compiler_params=params(),
    )(*parts, weight, upstream)


def backward_kernel(count, lists, first, capacity, list_ref, hold_ref, *refs):
    pay_refs, out_refs = refs[: -2 - count], refs[-2 - count : -2]
    total_ref, back_ref = refs[-2:]
    reps = len(pay_refs)
    rows = out_refs[0].shape[0]
    own = rows // reps
    per_slot = hold_ref.shape[0] // count
    codes = lists * capacity * BACKWARD_WIDTH
    ends = codes + lists * capacity
    place = ends + lists
    here = list_ref[place]
    for shift, pay_ref in enumerate(pay_refs):
        start = pl.multiple_of((here + reps - shift) % reps * own, own)
        back_ref[pl.ds(start, own), :] = pay_ref[:own, :]
    back_ref[rows:, :] = jnp.zeros((TILE, TILE), jnp.bfloat16)
    total_ref[...] = jnp.zeros_like(total_ref)
    for number in range(0, count, PAIR):
        listed = first + number // PAIR

        def product(group, listed=listed, number=number):
            begin = (listed * capacity + group) * BACKWARD_WIDTH
            items = [list_ref[begin + item] for item in range(BACKWARD_WIDTH)]
            starts = [pl.multiple_of(code % CODE * TILE, TILE) for code in items]
            left = jnp.concatenate([back_ref[pl.ds(start, TILE), :] for start in starts], axis=1)
            right = jnp.concatenate(
                [hold_ref[number * per_slot + code // CODE] for code in items], axis=0
            )
            return jnp.dot(left, right, preferred_element_type=jnp.float32)

        def target_of(group, listed=listed):
            return list_ref[codes + listed * capacity + group]

        def store(span, total):
            total_ref[span, :] = total.astype(jnp.bfloat16)

        group_turns(list_ref[ends + listed], BACKWARD_TURN, target_of, store, product)
        for item in range(PAIR):
            out_refs[number + item][...] = total_ref[item * rows : (item + 1) * rows, :]
        if number + PAIR < count:
            total_ref[...] = jnp.zeros_like(total_ref)


def backward_product(count, rows, lists, first, packed, capacity, held, pays):
    out_shape = jax.ShapeDtypeStruct((rows, TILE), jnp.bfloat16)
    return pl.pallas_call(
        functools.partial(backward_kernel, count, lists, first, capacity),
        out_shape=[out_shape] * count,
        grid_spec=pltpu.PrefetchScalarGridSpec(
            num_scalar_prefetch=1,
            grid=(),
            in_specs=[whole()] * (1 + len(pays)),
            out_specs=[whole()] * count,
            scratch_shapes=[
                pltpu.VMEM((PAIR * rows + TILE, TILE), jnp.bfloat16),
                pltpu.VMEM((rows + TILE, TILE), jnp.bfloat16),
            ],
        ),
        compiler_params=params(),
        cost_estimate=estimate(held.shape[0]),
    )(packed, held, *pays)


def restore_kernel(place_ref, order_ref, home_ref, *refs):
    out_refs, part_ref = refs[:-1], refs[-1]
    rows = order_ref.shape[1]
    reps = len(out_refs)
    own = rows // reps
    for block in range(rows // TILE):
        span = slice(block * TILE, (block + 1) * TILE)
        part_ref[span, :] = home_ref[span, :].astype(jnp.float32).T.astype(jnp.bfloat16)
    order = order_ref[...]
    part = part_ref[...]
    for shift, out_ref in enumerate(out_refs):
        start = (place_ref[0] + shift) % reps * own
        level = lax.broadcasted_iota(jnp.int32, (own, rows), 0) + start
        pick = (jnp.broadcast_to(order, (own, rows)) == level).astype(jnp.float32)
        out_ref[...] = jnp.dot(
            pick.astype(jnp.bfloat16), part, preferred_element_type=jnp.float32
        ).astype(jnp.bfloat16)


def restore(place, order, home, reps):
    rows = order.shape[1]
    out_shape = jax.ShapeDtypeStruct((rows // reps, TILE), jnp.bfloat16)
    return pl.pallas_call(
        restore_kernel,
        out_shape=[out_shape] * reps,
        grid_spec=pltpu.PrefetchScalarGridSpec(
            num_scalar_prefetch=1,
            grid=(),
            in_specs=[whole()] * 2,
            out_specs=[whole()] * reps,
            scratch_shapes=[pltpu.VMEM((rows, TILE), jnp.bfloat16)],
        ),
        compiler_params=params(),
    )(place, order, home)


def added(*values):
    return sum(value.astype(jnp.float32) for value in values).astype(jnp.bfloat16)


def per_device(features, node_order, adj_values, adj_rows, adj_cols, tile_count, weight, upstream):
    reps = lax.axis_size("rep")
    slices = lax.axis_size("blk")
    steps = slices // reps
    rows_dev = features.shape[0]
    blocks = rows_dev // TILE
    both = ("blk", "rep")
    row_ids, col_ids, counts = adj_rows[0, 0], adj_cols[0, 0], tile_count[0, 0]
    per_slot = row_ids.shape[1]
    tiles = adj_values.reshape((-1, TILE, TILE))
    own_rep = lax.axis_index("rep").astype(jnp.int32).reshape(1)

    here = lax.axis_index("blk") * reps + lax.axis_index("rep")
    slots = lax.dynamic_index_in_dim(jnp.asarray(slot_table()), here, 0, keepdims=False)
    place = jnp.concatenate([own_rep, slots])
    half = rows_dev // 2

    def moved(value, listed):
        return lax.ppermute(value, both, listed)

    def up(value):
        return moved(value, ring_pairs(1))

    def down(value):
        return moved(value, ring_pairs(-1))

    def swapped(value):
        return moved(value, partner_pairs())

    def to_reps(values):
        received = [values[0]]
        for shift in range(1, reps):
            along = [(rep, (rep + shift) % reps) for rep in range(reps)]
            received.append(lax.ppermute(values[shift], "rep", along))
        return received

    blocked = order_rows(node_order, features)
    near = moved(blocked, fetch_pairs())
    above, below = down(near), up(near)
    far = swapped(near)
    known, near = lax.optimization_barrier((place, near))
    held = [hold(FORWARD_WAVES[0], known, tiles, per_slot)]
    above, below, far, held[0] = lax.optimization_barrier((above, below, far, held[0]))
    middle = [down(above[:half]), up(below[half:])]
    known, far = lax.optimization_barrier((place, far))
    held.append(hold(FORWARD_WAVES[1], known, tiles, per_slot))
    arrived = {0: [near], 1: [above], 2: middle, 3: [below], 4: [far], 5: [swapped(above)]}
    arrived[6] = [swapped(value) for value in middle]
    arrived[7] = [swapped(below)]
    alive = jnp.arange(per_slot, dtype=jnp.int32)[None, :] < counts[:, None]
    cells = jnp.take(jnp.where(alive, row_ids * CODE + col_ids, -1), slots, axis=0)

    def split(cells, items):
        chosen = jnp.concatenate([cells[item : item + 1] for item in items])
        return chosen >= 0, chosen // CODE, chosen % CODE

    waves = len(FORWARD_WAVES)
    alive, rows_of, cols_of = split(cells, sum(FORWARD_WAVES, ()))
    offsets = jnp.arange(steps, dtype=jnp.int32)[:, None] % (steps // waves) * blocks
    packed, capacity = tile_lists(
        jnp.where(alive, rows_of, blocks).reshape(waves, -1),
        (cols_of + offsets).reshape(waves, -1),
        blocks,
        steps // waves * blocks,
        FORWARD_WIDTH,
        FORWARD_TURN,
    )
    packed = jnp.concatenate([packed, own_rep])
    total = None
    for wave, items in enumerate(FORWARD_WAVES):
        xs = sum([arrived[item] for item in items], [])
        total = forward_product(
            rows_dev, waves, wave, packed, capacity, held[wave], xs, total, reps
        )
    total = list(total)
    last_cells, total[0] = lax.optimization_barrier((cells, total[0]))
    shared = to_reps(total)
    lists = steps // PAIR
    alive, rows_of, cols_of = split(last_cells, sum(BACKWARD_WAVES, ()))
    offsets = jnp.arange(steps, dtype=jnp.int32)[:, None] % PAIR * blocks
    packed, capacity = tile_lists(
        jnp.where(alive, cols_of + offsets, PAIR * blocks).reshape(lists, -1),
        rows_of.reshape(lists, -1),
        PAIR * blocks,
        blocks,
        BACKWARD_WIDTH,
        BACKWARD_TURN,
    )
    packed = jnp.concatenate([packed, own_rep])
    shared[1], packed = lax.optimization_barrier((shared[1], packed))
    activations, pay = dense_layer(shared, weight, upstream)
    late_place, pay = lax.optimization_barrier((place, pay))
    pays = to_reps([pay] * reps)
    holds = [hold(items, late_place, tiles, per_slot) for items in BACKWARD_WAVES]
    packed, holds = lax.optimization_barrier((packed, holds))

    def products(wave, packed):
        count = len(BACKWARD_WAVES[wave])
        first = wave * count // PAIR
        return list(
            backward_product(count, rows_dev, lists, first, packed, capacity, holds[wave], pays)
        )

    grad_weight = sum(pay[-weight.size // TILE :].astype(jnp.float32) for pay in pays)
    todo = blk_steps()

    def next_after(total, value):
        total, value = lax.optimization_barrier((total, value))
        return total + moved(total, todo.pop(0)), value

    step = moved(grad_weight, todo.pop(0))
    others = products(0, packed)
    step, packed, others[0] = lax.optimization_barrier((step, packed, others[0]))
    grad_weight = grad_weight + step
    returned = {item: swapped(others[item]) for item in (2, 1, 3, 0)}
    mine = products(1, packed)
    two = added(mine[2], returned[2])
    from_below, from_above = lax.optimization_barrier((up(two[:half]), down(two[half:])))
    grad_weight, returned[1] = next_after(grad_weight, returned[1])
    one = jnp.concatenate(
        [added(mine[1][:half], returned[1][:half], from_below), added(mine[1][half:], returned[1][half:])]
    )
    three = jnp.concatenate(
        [added(mine[3][:half], returned[3][:half]), added(mine[3][half:], returned[3][half:], from_above)]
    )
    onward = [up(one), down(three)]
    ended = added(mine[0], returned[0], *onward)
    grad_weight, ended = next_after(grad_weight, ended)
    home = moved(ended, [(user, owner) for owner, user in fetch_pairs()])
    grad_weight, home = next_after(grad_weight, home)
    grad_weight = grad_weight + moved(grad_weight, todo.pop(0))
    terms = to_reps(restore(own_rep, node_order, home, reps))
    grad_features = added(*terms)
    stacked = grad_weight.reshape(weight.shape[1] // TILE, weight.shape[0], TILE)
    grad_weight = jnp.concatenate([stacked[half] for half in range(stacked.shape[0])], axis=1)
    return (activations, grad_weight, grad_features)


def solution(mesh):
    placed = (
        P("blk", None),
        P("blk", None),
        P("blk", "rep", None, None, None, None),
        P("blk", "rep", None, None),
        P("blk", "rep", None, None),
        P("blk", "rep", None),
        P(),
        P(("blk", "rep"), None),
    )
    return jax.shard_map(
        per_device,
        mesh=mesh,
        in_specs=placed,
        out_specs=(P(("blk", "rep"), None), P(), P(("blk", "rep"), None)),
        check_vma=False,
    )
```

```python
import functools

import jax
import jax.numpy as jnp
import numpy as np
from jax import lax
from jax.experimental import pallas as pl
from jax.experimental.pallas import tpu as pltpu
from jax.sharding import PartitionSpec as P

TILE = 128
FORWARD_TURN = 4
BACKWARD_TURN = 8
FORWARD_WIDTH = 8
BACKWARD_WIDTH = 4
FORWARD_WAVES = ((0, 1, 3, 2), (4, 5, 7, 6))
BACKWARD_WAVES = ((6, 5, 7, 4), (0, 1, 2, 3))
BACKWARD_OUTPUTS = ((1, 2, 1), (1, 1, 1, 1))
PAIR = 2
PARTS = 4
CODE = 256
VMEM_LIMIT = 12 * 1024 * 1024
HOLD_LIMIT = 32 * 1024 * 1024
STREAM_LIMIT = 40 * 1024 * 1024


def spots():
    return [(x, y, z, c) for x in range(4) for y in range(4) for z in range(4) for c in range(2)]


def coords(x, y, z, c):
    return 8 * y + 2 * z + x % 2, x // 2 * 2 + c


def device(x, y, z, c):
    blk, rep = coords(x % 4, y % 4, z % 4, c)
    return 4 * blk + rep


def levels(x, y, z, c):
    kind = sum(coords(x, y, z, c)) % 4
    level = z if kind // 2 == z % 2 else z + 1
    return kind % 2, (level + 2 * c) % 4, (level + 2 - 2 * c) % 4


def slot_table():
    table = np.zeros((128, 8), np.int32)
    for spot in spots():
        low, near, far = levels(*spot)
        base = sum(coords(*spot))
        for item in range(8):
            row = (spot[1] + item) % 4
            wanted = 8 * row + 2 * (near if item < 4 else far) + low
            table[device(*spot), item] = (wanted - base) % 32 // 4
    return table


def fetch_pairs():
    listed = []
    for x, y, z, c in spots():
        near = levels(x, y, z, c)[1]
        listed.append((device(x - c, y, near, c), device(x, y, z, c)))
    return listed


def partner_pairs():
    return [(device(x, y, z, c), device(x + 2 * c - 1, y, z, 1 - c)) for x, y, z, c in spots()]


def ring_pairs(step):
    return [(device(x, y, z, c), device(x, y + step, z, c)) for x, y, z, c in spots()]


def params(limit=VMEM_LIMIT):
    return pltpu.CompilerParams(vmem_limit_bytes=limit)


def whole():
    return pl.BlockSpec(memory_space=pltpu.VMEM)


def order_kernel(order_ref, feat_ref, out_ref):
    rows = feat_ref.shape[0]
    step = 512
    feats = feat_ref[...]
    for start in range(0, rows, step):
        parts = []
        for inner in range(start, start + step, TILE):
            line = order_ref[0:1, inner : inner + TILE]
            parts.append(jnp.broadcast_to(line, (TILE, TILE)).T)
        column = jnp.concatenate(parts, axis=0)
        pieces = []
        for col in range(0, rows, TILE):
            level = lax.broadcasted_iota(jnp.int32, (step, TILE), 1) + col
            pieces.append((column == level).astype(jnp.float32).astype(jnp.bfloat16))
        pick = jnp.concatenate(pieces, axis=1)
        out_ref[start : start + step, :] = jnp.dot(
            pick, feats, preferred_element_type=jnp.float32
        ).astype(jnp.bfloat16)


def order_rows(order, features):
    return pl.pallas_call(
        order_kernel,
        out_shape=jax.ShapeDtypeStruct(features.shape, jnp.bfloat16),
        in_specs=[whole(), whole()],
        out_specs=whole(),
        compiler_params=params(),
    )(order, features)


def tile_copies(slots, tiles_ref, out_ref, sems):
    per_slot = out_ref.shape[0] // len(slots)
    part = per_slot // PARTS
    copies = []
    for number, slot in enumerate(slots):
        for piece in range(PARTS):
            target = number * per_slot + piece * part
            copies.append(
                pltpu.make_async_copy(
                    tiles_ref.at[pl.ds(slot * per_slot + piece * part, part)],
                    out_ref.at[pl.ds(target, part)],
                    sems.at[number * PARTS + piece],
                )
            )
    return copies


def hold_kernel(items, place_ref, tiles_ref, out_ref, sems):
    slots = [place_ref[1 + item] for item in items]
    copies = tile_copies(slots, tiles_ref, out_ref, sems)
    for copy in copies:
        copy.start()
    for copy in copies:
        copy.wait()


def hold(items, place, tiles, per_slot):
    size = len(items) * per_slot
    return pl.pallas_call(
        functools.partial(hold_kernel, items),
        out_shape=jax.ShapeDtypeStruct((size, TILE, TILE), tiles.dtype),
        grid_spec=pltpu.PrefetchScalarGridSpec(
            num_scalar_prefetch=1,
            grid=(),
            in_specs=[pl.BlockSpec(memory_space=pltpu.HBM)],
            out_specs=whole(),
            scratch_shapes=[pltpu.SemaphoreType.DMA((len(items) * PARTS,))],
        ),
        compiler_params=params(HOLD_LIMIT),
        cost_estimate=pl.CostEstimate(
            flops=0, bytes_accessed=4 * size * TILE * TILE, transcendentals=0
        ),
    )(place, tiles)


def tile_lists(key, source, target_count, zero, width, turn):
    lists, size = key.shape
    capacity = (size + target_count * (width - 1)) // width
    capacity = -(-capacity // turn) * turn
    ids = jnp.arange(size, dtype=jnp.int32)
    levels = jnp.arange(target_count, dtype=jnp.int32)
    earlier = (key[:, None, :] == key[:, :, None]) & (ids[None, :] < ids[:, None])
    rank = jnp.sum(earlier.astype(jnp.int32), axis=2)
    held = jnp.sum((key[:, None, :] == levels[:, None]).astype(jnp.int32), axis=2)
    needed = (held + width - 1) // width
    upto = levels[None, :] <= levels[:, None]
    ends = jnp.sum(jnp.where(upto, needed[:, None, :], 0), axis=2)
    base = jnp.sum(jnp.where(levels < key[:, :, None], needed[:, None, :], 0), axis=2)
    place = jnp.where(key < target_count, base * width + rank, -1)
    cells = jnp.arange(capacity * width, dtype=jnp.int32)
    hit = (place[:, None, :] == cells[:, None]).astype(jnp.int32)
    tile = jnp.sum(hit * ids, axis=2)
    origin = zero + jnp.sum(hit * (source - zero)[:, None, :], axis=2)
    groups = jnp.arange(capacity, dtype=jnp.int32)
    target = jnp.sum((ends[:, None, :] <= groups[:, None]).astype(jnp.int32), axis=2)
    code = tile * CODE + origin
    packed = jnp.concatenate([code.reshape(-1), target.reshape(-1), jnp.max(ends, axis=1)])
    return packed, capacity


def group_turns(groups, length, target_of, store, product):
    def turn(index, total):
        for lane in range(length):
            group = index * length + lane
            target = target_of(group)
            new = (group == 0) | (target != target_of(jnp.maximum(group - 1, 0)))
            fresh = product(group)
            total = jnp.where(new, fresh, total + fresh)
            store(pl.ds(pl.multiple_of(target * TILE, TILE), TILE), total)
        return total

    turns = (groups + length - 1) // length
    lax.fori_loop(0, turns, turn, jnp.zeros((TILE, TILE), jnp.float32))


def forward_kernel(pieces, lists, wave, capacity, list_ref, hold_ref, *refs):
    first = wave == 0
    x_refs, refs = refs[:pieces], refs[pieces:]
    codes = lists * capacity * FORWARD_WIDTH
    ends = codes + lists * capacity
    copies = []
    if first:
        tiles_ref = hold_ref
        total_ref, x_ref, hold_ref, sems = refs
        slots = [list_ref[ends + lists + 1 + item] for item in FORWARD_WAVES[0]]
        copies = tile_copies(slots, tiles_ref, hold_ref, sems)
        for copy in copies:
            copy.start()
        total_ref[...] = jnp.zeros_like(total_ref)
    else:
        before_ref, out_refs, (total_ref, x_ref) = refs[0], refs[1:-2], refs[-2:]
        total_ref[...] = before_ref[...].astype(jnp.bfloat16)
    start = 0
    for piece_ref in x_refs:
        x_ref[start : start + piece_ref.shape[0], :] = piece_ref[...]
        start += piece_ref.shape[0]
    x_ref[start:, :] = jnp.zeros((TILE, TILE), jnp.bfloat16)
    for copy in copies:
        copy.wait()

    def product(group):
        begin = (wave * capacity + group) * FORWARD_WIDTH
        codes = [list_ref[begin + item] for item in range(FORWARD_WIDTH)]
        left = jnp.concatenate([hold_ref[code // CODE] for code in codes], axis=1)
        starts = [pl.multiple_of(code % CODE * TILE, TILE) for code in codes]
        right = jnp.concatenate([x_ref[pl.ds(start, TILE), :] for start in starts], axis=0)
        return jnp.dot(left, right, preferred_element_type=jnp.float32)

    def store(span, total):
        if first:
            total_ref[span, :] = total
        else:
            total_ref[span, :] = (total + before_ref[span, :]).astype(jnp.bfloat16)

    group_turns(
        list_ref[ends + wave],
        FORWARD_TURN,
        lambda group: list_ref[codes + wave * capacity + group],
        store,
        product,
    )
    if not first:
        reps = len(out_refs)
        own = out_refs[0].shape[0]
        here = list_ref[ends + lists]
        for shift, out_ref in enumerate(out_refs):
            start = pl.multiple_of((here + shift) % reps * own, own)
            out_ref[...] = total_ref[pl.ds(start, own), :]


def estimate(tiles):
    return pl.CostEstimate(
        flops=8 * tiles * TILE**3, bytes_accessed=tiles * TILE * TILE * 2, transcendentals=0
    )


def forward_product(rows, lists, wave, packed, capacity, tiles, xs, before, reps):
    first = wave == 0
    total_shape = (rows + TILE, TILE)
    x_rows = sum(x.shape[0] for x in xs)
    x_scratch = pltpu.VMEM((x_rows + TILE, TILE), jnp.bfloat16)
    in_specs = [whole()] * (1 + len(xs))
    if first:
        operands = [tiles, *xs]
        in_specs[0] = pl.BlockSpec(memory_space=pltpu.HBM)
        out_shape = jax.ShapeDtypeStruct(total_shape, jnp.float32)
        out_specs = whole()
        count = len(FORWARD_WAVES[0])
        held = (tiles.shape[0] // (lists * count) * count, TILE, TILE)
        scratch = [
            x_scratch,
            pltpu.VMEM(held, jnp.bfloat16),
            pltpu.SemaphoreType.DMA((count * PARTS,)),
        ]
    else:
        operands = [tiles, *xs, before]
        in_specs.append(whole())
        out_shape = [jax.ShapeDtypeStruct((rows // reps, TILE), jnp.bfloat16)] * reps
        out_specs = [whole()] * reps
        scratch = [pltpu.VMEM(total_shape, jnp.bfloat16), x_scratch]
    return pl.pallas_call(
        functools.partial(forward_kernel, len(xs), lists, wave, capacity),
        out_shape=out_shape,
        grid_spec=pltpu.PrefetchScalarGridSpec(
            num_scalar_prefetch=1,
            grid=(),
            in_specs=in_specs,
            out_specs=out_specs,
            scratch_shapes=scratch,
        ),
        compiler_params=params(STREAM_LIMIT if first else VMEM_LIMIT),
        cost_estimate=estimate(x_rows // rows * 80),
    )(packed, *operands)


def dense_kernel(*refs):
    part_refs, (weight_ref, upstream_ref, act_ref, pay_ref) = refs[:-4], refs[-4:]
    rows = upstream_ref.shape[0]
    total = part_refs[0][...].astype(jnp.float32)
    for part_ref in part_refs[1:]:
        total = total + part_ref[...].astype(jnp.float32)
    aggregated = total.astype(jnp.bfloat16)
    weight = weight_ref[...]
    pre = jnp.dot(aggregated, weight, preferred_element_type=jnp.float32)
    gate = jax.nn.sigmoid(pre)
    act_ref[...] = (pre * gate).astype(jnp.bfloat16)
    grad_pre = (
        upstream_ref[...].astype(jnp.float32) * gate * (1.0 + pre * (1.0 - gate))
    ).astype(jnp.bfloat16)
    back = lax.dot_general(
        weight, grad_pre, (((1,), (1,)), ((), ())), preferred_element_type=jnp.float32
    ).astype(jnp.bfloat16)
    for block in range(rows // TILE):
        pay_ref[block * TILE : (block + 1) * TILE, :] = back[:, block * TILE : (block + 1) * TILE]
    local = lax.dot_general(
        aggregated, grad_pre, (((0,), (0,)), ((), ())), preferred_element_type=jnp.float32
    ).astype(jnp.bfloat16)
    for half in range(weight.shape[1] // TILE):
        pay_ref[rows + half * TILE : rows + (half + 1) * TILE, :] = local[
            :, half * TILE : (half + 1) * TILE
        ]


def dense_layer(parts, weight, upstream):
    rows, hidden = upstream.shape
    pay_rows = rows + hidden // TILE * weight.shape[0]
    return pl.pallas_call(
        dense_kernel,
        out_shape=(
            jax.ShapeDtypeStruct((rows, hidden), jnp.bfloat16),
            jax.ShapeDtypeStruct((pay_rows, TILE), jnp.bfloat16),
        ),
        in_specs=[whole()] * (len(parts) + 2),
        out_specs=(whole(), whole()),
        compiler_params=params(),
    )(*parts, weight, upstream)


def backward_kernel(sizes, rows, lists, first, capacity, list_ref, hold_ref, *refs):
    pay_refs, out_refs = refs[: -2 - len(sizes)], refs[-2 - len(sizes) : -2]
    count = sum(sizes)
    spots_of = [(number, item) for number, size in enumerate(sizes) for item in range(size)]
    total_ref, back_ref = refs[-2:]
    reps = len(pay_refs)
    own = rows // reps
    per_slot = hold_ref.shape[0] // count
    codes = lists * capacity * BACKWARD_WIDTH
    ends = codes + lists * capacity
    place = ends + lists
    here = list_ref[place]
    for shift, pay_ref in enumerate(pay_refs):
        start = pl.multiple_of((here + reps - shift) % reps * own, own)
        back_ref[pl.ds(start, own), :] = pay_ref[:own, :]
    back_ref[rows:, :] = jnp.zeros((TILE, TILE), jnp.bfloat16)
    total_ref[...] = jnp.zeros_like(total_ref)
    if out_refs[0].shape[0] > sizes[0] * rows:
        ride = pay_refs[0][own:, :].astype(jnp.float32)
        for pay_ref in pay_refs[1:]:
            ride = ride + pay_ref[own:, :].astype(jnp.float32)
        out_refs[0][sizes[0] * rows :, :] = ride.astype(jnp.bfloat16)
    for number in range(0, count, PAIR):
        listed = first + number // PAIR

        def product(group, listed=listed, number=number):
            begin = (listed * capacity + group) * BACKWARD_WIDTH
            items = [list_ref[begin + item] for item in range(BACKWARD_WIDTH)]
            starts = [pl.multiple_of(code % CODE * TILE, TILE) for code in items]
            left = jnp.concatenate([back_ref[pl.ds(start, TILE), :] for start in starts], axis=1)
            right = jnp.concatenate(
                [hold_ref[number * per_slot + code // CODE] for code in items], axis=0
            )
            return jnp.dot(left, right, preferred_element_type=jnp.float32)

        def target_of(group, listed=listed):
            return list_ref[codes + listed * capacity + group]

        def store(span, total):
            total_ref[span, :] = total.astype(jnp.bfloat16)

        group_turns(list_ref[ends + listed], BACKWARD_TURN, target_of, store, product)
        for item in range(PAIR):
            target, spot = spots_of[number + item]
            out_refs[target][spot * rows : (spot + 1) * rows, :] = total_ref[
                item * rows : (item + 1) * rows, :
            ]
        if number + PAIR < count:
            total_ref[...] = jnp.zeros_like(total_ref)


def backward_product(sizes, rows, lists, first, packed, capacity, held, pays):
    out_rows = [size * rows for size in sizes]
    if first == 0:
        out_rows[0] += pays[0].shape[0] - rows // len(pays)
    return pl.pallas_call(
        functools.partial(backward_kernel, sizes, rows, lists, first, capacity),
        out_shape=[jax.ShapeDtypeStruct((size, TILE), jnp.bfloat16) for size in out_rows],
        grid_spec=pltpu.PrefetchScalarGridSpec(
            num_scalar_prefetch=1,
            grid=(),
            in_specs=[whole()] * (1 + len(pays)),
            out_specs=[whole()] * len(sizes),
            scratch_shapes=[
                pltpu.VMEM((PAIR * rows + TILE, TILE), jnp.bfloat16),
                pltpu.VMEM((rows + TILE, TILE), jnp.bfloat16),
            ],
        ),
        compiler_params=params(),
        cost_estimate=estimate(held.shape[0]),
    )(packed, held, *pays)


def restore_kernel(place_ref, order_ref, home_ref, *refs):
    out_refs, part_ref = refs[:-1], refs[-1]
    rows = order_ref.shape[1]
    reps = len(out_refs)
    own = rows // reps
    for block in range(rows // TILE):
        span = slice(block * TILE, (block + 1) * TILE)
        part_ref[span, :] = home_ref[span, :].astype(jnp.float32).T.astype(jnp.bfloat16)
    order = order_ref[...]
    part = part_ref[...]
    for shift, out_ref in enumerate(out_refs):
        start = (place_ref[0] + shift) % reps * own
        level = lax.broadcasted_iota(jnp.int32, (own, rows), 0) + start
        pick = (jnp.broadcast_to(order, (own, rows)) == level).astype(jnp.float32)
        out_ref[:own, :] = jnp.dot(
            pick.astype(jnp.bfloat16), part, preferred_element_type=jnp.float32
        ).astype(jnp.bfloat16)
        out_ref[own:, :] = home_ref[rows:, :]


def restore(place, order, home, reps):
    rows = order.shape[1]
    out_rows = rows // reps + home.shape[0] - rows
    out_shape = jax.ShapeDtypeStruct((out_rows, TILE), jnp.bfloat16)
    return pl.pallas_call(
        restore_kernel,
        out_shape=[out_shape] * reps,
        grid_spec=pltpu.PrefetchScalarGridSpec(
            num_scalar_prefetch=1,
            grid=(),
            in_specs=[whole()] * 2,
            out_specs=[whole()] * reps,
            scratch_shapes=[pltpu.VMEM((rows, TILE), jnp.bfloat16)],
        ),
        compiler_params=params(),
    )(place, order, home)


def added(*values):
    return sum(value.astype(jnp.float32) for value in values).astype(jnp.bfloat16)


def per_device(features, node_order, adj_values, adj_rows, adj_cols, tile_count, weight, upstream):
    reps = lax.axis_size("rep")
    slices = lax.axis_size("blk")
    steps = slices // reps
    rows_dev = features.shape[0]
    blocks = rows_dev // TILE
    both = ("blk", "rep")
    row_ids, col_ids, counts = adj_rows[0, 0], adj_cols[0, 0], tile_count[0, 0]
    per_slot = row_ids.shape[1]
    tiles = adj_values.reshape((-1, TILE, TILE))
    own_rep = lax.axis_index("rep").astype(jnp.int32).reshape(1)

    here = lax.axis_index("blk") * reps + lax.axis_index("rep")
    slots = lax.dynamic_index_in_dim(jnp.asarray(slot_table()), here, 0, keepdims=False)
    place = jnp.concatenate([own_rep, slots])
    half = rows_dev // 2

    def moved(value, listed):
        return lax.ppermute(value, both, listed)

    def up(value):
        return moved(value, ring_pairs(1))

    def down(value):
        return moved(value, ring_pairs(-1))

    def swapped(value):
        return moved(value, partner_pairs())

    def to_reps(values):
        received = [values[0]]
        for shift in range(1, reps):
            along = [(rep, (rep + shift) % reps) for rep in range(reps)]
            received.append(lax.ppermute(values[shift], "rep", along))
        return received

    blocked = order_rows(node_order, features)
    near = moved(blocked, fetch_pairs())
    alive = jnp.arange(per_slot, dtype=jnp.int32)[None, :] < counts[:, None]
    cells = jnp.take(jnp.where(alive, row_ids * CODE + col_ids, -1), slots, axis=0)

    def split(cells, items):
        chosen = jnp.concatenate([cells[item : item + 1] for item in items])
        return chosen >= 0, chosen // CODE, chosen % CODE

    waves = len(FORWARD_WAVES)
    alive, rows_of, cols_of = split(cells, sum(FORWARD_WAVES, ()))
    offsets = jnp.arange(steps, dtype=jnp.int32)[:, None] % (steps // waves) * blocks
    forward_list, forward_capacity = tile_lists(
        jnp.where(alive, rows_of, blocks).reshape(waves, -1),
        (cols_of + offsets).reshape(waves, -1),
        blocks,
        steps // waves * blocks,
        FORWARD_WIDTH,
        FORWARD_TURN,
    )
    forward_list = jnp.concatenate([forward_list, place])
    late_cells, near = lax.optimization_barrier((cells, near))
    lists = steps // PAIR
    alive, rows_of, cols_of = split(late_cells, sum(BACKWARD_WAVES, ()))
    offsets = jnp.arange(steps, dtype=jnp.int32)[:, None] % PAIR * blocks
    packed, capacity = tile_lists(
        jnp.where(alive, cols_of + offsets, PAIR * blocks).reshape(lists, -1),
        rows_of.reshape(lists, -1),
        PAIR * blocks,
        blocks,
        BACKWARD_WIDTH,
        BACKWARD_TURN,
    )
    packed = jnp.concatenate([packed, own_rep])
    above, below = down(near), up(near)
    far = swapped(near)
    above, below, far, forward_list, packed = lax.optimization_barrier(
        (above, below, far, forward_list, packed)
    )
    middle = [down(above[:half]), up(below[half:])]
    known, far = lax.optimization_barrier((place, far))
    held = hold(FORWARD_WAVES[1], known, tiles, per_slot)
    xs = [near, above, below, *middle]
    total = forward_product(
        rows_dev, waves, 0, forward_list, forward_capacity, tiles, xs, None, reps
    )
    xs = [far, swapped(above), swapped(below), *[swapped(value) for value in middle]]
    total = list(
        forward_product(
            rows_dev, waves, 1, forward_list, forward_capacity, held, xs, total, reps
        )
    )
    known, total[0] = lax.optimization_barrier((place, total[0]))
    shared = to_reps(total)
    holds = [hold(BACKWARD_WAVES[0], known, tiles, per_slot)]
    shared[1], holds[0] = lax.optimization_barrier((shared[1], holds[0]))
    activations, pay = dense_layer(shared, weight, upstream)
    known, pay = lax.optimization_barrier((place, pay))
    pays = to_reps([pay] * reps)
    holds.append(hold(BACKWARD_WAVES[1], known, tiles, per_slot))
    packed, holds = lax.optimization_barrier((packed, holds))

    def products(wave, packed):
        sizes = BACKWARD_OUTPUTS[wave]
        first = wave * sum(sizes) // PAIR
        return list(
            backward_product(sizes, rows_dev, lists, first, packed, capacity, holds[wave], pays)
        )

    others = products(0, packed)
    packed, others[2] = lax.optimization_barrier((packed, others[2]))
    returned = swapped(others[0])
    sides = swapped(others[1])
    last = swapped(others[2])
    mine = products(1, packed)
    two = added(mine[2], returned[:rows_dev])
    ride = added(others[0][rows_dev:], returned[rows_dev:])
    from_below, from_above = lax.optimization_barrier(
        (up(jnp.concatenate([two[:half], ride])), down(jnp.concatenate([two[half:], ride])))
    )
    one = jnp.concatenate(
        [
            added(mine[1][:half], sides[:half], from_below[:half]),
            added(mine[1][half:], sides[half:rows_dev]),
            from_below[half:],
        ]
    )
    three = jnp.concatenate(
        [
            added(mine[3][:half], sides[rows_dev : rows_dev + half]),
            added(mine[3][half:], sides[rows_dev + half :], from_above[:half]),
        ]
    )
    below_sum, above_sum = up(one), down(three)
    ended = jnp.concatenate(
        [
            added(mine[0], last, below_sum[:rows_dev], above_sum),
            added(ride, from_below[half:], from_above[half:], below_sum[rows_dev:]),
        ]
    )
    home = moved(ended, [(user, owner) for owner, user in fetch_pairs()])
    terms = to_reps(restore(own_rep, node_order, home, reps))
    own = rows_dev // reps
    grad_features = added(*[term[:own] for term in terms])
    grad_weight = sum(term[own:].astype(jnp.float32) for term in terms)
    stacked = grad_weight.reshape(weight.shape[1] // TILE, weight.shape[0], TILE)
    grad_weight = jnp.concatenate([stacked[half] for half in range(stacked.shape[0])], axis=1)
    return (activations, grad_weight, grad_features)


def solution(mesh):
    placed = (
        P("blk", None),
        P("blk", None),
        P("blk", "rep", None, None, None, None),
        P("blk", "rep", None, None),
        P("blk", "rep", None, None),
        P("blk", "rep", None),
        P(),
        P(("blk", "rep"), None),
    )
    return jax.shard_map(
        per_device,
        mesh=mesh,
        in_specs=placed,
        out_specs=(P(("blk", "rep"), None), P(), P(("blk", "rep"), None)),
        check_vma=False,
    )
```

```python
import functools

import jax
import jax.numpy as jnp
import numpy as np
from jax import lax
from jax.experimental import pallas as pl
from jax.experimental.pallas import tpu as pltpu
from jax.sharding import PartitionSpec as P

TILE = 128
FORWARD_TURN = 4
BACKWARD_TURN = 8
FORWARD_WIDTH = 8
BACKWARD_WIDTH = 4
FORWARD_WAVES = ((0, 1, 3, 2), (4, 5, 7, 6))
BACKWARD_WAVES = ((6, 5, 7, 4), (0, 1, 2, 3))
BACKWARD_OUTPUTS = ((1, 2, 1), (1, 1, 1, 1))
PAIR = 2
PARTS = 4
CODE = 256
VMEM_LIMIT = 12 * 1024 * 1024
HOLD_LIMIT = 32 * 1024 * 1024
STREAM_LIMIT = 40 * 1024 * 1024


def spots():
    return [(x, y, z, c) for x in range(4) for y in range(4) for z in range(4) for c in range(2)]


def coords(x, y, z, c):
    return 8 * y + 2 * z + x % 2, x // 2 * 2 + c


def device(x, y, z, c):
    blk, rep = coords(x % 4, y % 4, z % 4, c)
    return 4 * blk + rep


def levels(x, y, z, c):
    kind = sum(coords(x, y, z, c)) % 4
    level = z if kind // 2 == z % 2 else z + 1
    return kind % 2, (level + 2 * c) % 4, (level + 2 - 2 * c) % 4


def slot_table():
    table = np.zeros((128, 8), np.int32)
    for spot in spots():
        low, near, far = levels(*spot)
        base = sum(coords(*spot))
        for item in range(8):
            row = (spot[1] + item) % 4
            wanted = 8 * row + 2 * (near if item < 4 else far) + low
            table[device(*spot), item] = (wanted - base) % 32 // 4
    return table


def fetch_pairs():
    listed = []
    for x, y, z, c in spots():
        near = levels(x, y, z, c)[1]
        listed.append((device(x - c, y, near, c), device(x, y, z, c)))
    return listed


def fetched_rep(x, y, z, c):
    return coords((x - c) % 4, y, z, c)[1]


def quarter_pairs(shift):
    listed = []
    for x, y, z, c in spots():
        near = levels(x, y, z, c)[1]
        blk = device(x - c, y, near, c) // 4
        listed.append((device(x, y, z, c), 4 * blk + (fetched_rep(x, y, z, c) + shift) % 4))
    return listed


def rep_table():
    table = np.zeros((128, 1), np.int32)
    for spot in spots():
        table[device(*spot), 0] = fetched_rep(*spot)
    return table


def partner_pairs():
    return [(device(x, y, z, c), device(x + 2 * c - 1, y, z, 1 - c)) for x, y, z, c in spots()]


def ring_pairs(step):
    return [(device(x, y, z, c), device(x, y + step, z, c)) for x, y, z, c in spots()]


def params(limit=VMEM_LIMIT):
    return pltpu.CompilerParams(vmem_limit_bytes=limit)


def whole():
    return pl.BlockSpec(memory_space=pltpu.VMEM)


def order_kernel(order_ref, feat_ref, out_ref):
    rows = feat_ref.shape[0]
    step = 512
    feats = feat_ref[...]
    for start in range(0, rows, step):
        parts = []
        for inner in range(start, start + step, TILE):
            line = order_ref[0:1, inner : inner + TILE]
            parts.append(jnp.broadcast_to(line, (TILE, TILE)).T)
        column = jnp.concatenate(parts, axis=0)
        pieces = []
        for col in range(0, rows, TILE):
            level = lax.broadcasted_iota(jnp.int32, (step, TILE), 1) + col
            pieces.append((column == level).astype(jnp.float32).astype(jnp.bfloat16))
        pick = jnp.concatenate(pieces, axis=1)
        out_ref[start : start + step, :] = jnp.dot(
            pick, feats, preferred_element_type=jnp.float32
        ).astype(jnp.bfloat16)


def order_rows(order, features):
    return pl.pallas_call(
        order_kernel,
        out_shape=jax.ShapeDtypeStruct(features.shape, jnp.bfloat16),
        in_specs=[whole(), whole()],
        out_specs=whole(),
        compiler_params=params(),
    )(order, features)


def tile_copies(slots, tiles_ref, out_ref, sems):
    per_slot = out_ref.shape[0] // len(slots)
    part = per_slot // PARTS
    copies = []
    for number, slot in enumerate(slots):
        for piece in range(PARTS):
            target = number * per_slot + piece * part
            copies.append(
                pltpu.make_async_copy(
                    tiles_ref.at[pl.ds(slot * per_slot + piece * part, part)],
                    out_ref.at[pl.ds(target, part)],
                    sems.at[number * PARTS + piece],
                )
            )
    return copies


def hold_kernel(items, place_ref, tiles_ref, out_ref, sems):
    slots = [place_ref[1 + item] for item in items]
    copies = tile_copies(slots, tiles_ref, out_ref, sems)
    for copy in copies:
        copy.start()
    for copy in copies:
        copy.wait()


def hold(items, place, tiles, per_slot):
    size = len(items) * per_slot
    return pl.pallas_call(
        functools.partial(hold_kernel, items),
        out_shape=jax.ShapeDtypeStruct((size, TILE, TILE), tiles.dtype),
        grid_spec=pltpu.PrefetchScalarGridSpec(
            num_scalar_prefetch=1,
            grid=(),
            in_specs=[pl.BlockSpec(memory_space=pltpu.HBM)],
            out_specs=whole(),
            scratch_shapes=[pltpu.SemaphoreType.DMA((len(items) * PARTS,))],
        ),
        compiler_params=params(HOLD_LIMIT),
        cost_estimate=pl.CostEstimate(
            flops=0, bytes_accessed=4 * size * TILE * TILE, transcendentals=0
        ),
    )(place, tiles)


def tile_lists(key, source, target_count, zero, width, turn):
    lists, size = key.shape
    capacity = (size + target_count * (width - 1)) // width
    capacity = -(-capacity // turn) * turn
    ids = jnp.arange(size, dtype=jnp.int32)
    levels = jnp.arange(target_count, dtype=jnp.int32)
    earlier = (key[:, None, :] == key[:, :, None]) & (ids[None, :] < ids[:, None])
    rank = jnp.sum(earlier.astype(jnp.int32), axis=2)
    held = jnp.sum((key[:, None, :] == levels[:, None]).astype(jnp.int32), axis=2)
    needed = (held + width - 1) // width
    upto = levels[None, :] <= levels[:, None]
    ends = jnp.sum(jnp.where(upto, needed[:, None, :], 0), axis=2)
    base = jnp.sum(jnp.where(levels < key[:, :, None], needed[:, None, :], 0), axis=2)
    place = jnp.where(key < target_count, base * width + rank, -1)
    cells = jnp.arange(capacity * width, dtype=jnp.int32)
    hit = (place[:, None, :] == cells[:, None]).astype(jnp.int32)
    tile = jnp.sum(hit * ids, axis=2)
    origin = zero + jnp.sum(hit * (source - zero)[:, None, :], axis=2)
    groups = jnp.arange(capacity, dtype=jnp.int32)
    target = jnp.sum((ends[:, None, :] <= groups[:, None]).astype(jnp.int32), axis=2)
    code = tile * CODE + origin
    packed = jnp.concatenate([code.reshape(-1), target.reshape(-1), jnp.max(ends, axis=1)])
    return packed, capacity


def group_turns(groups, length, target_of, store, product):
    def turn(index, total):
        for lane in range(length):
            group = index * length + lane
            target = target_of(group)
            new = (group == 0) | (target != target_of(jnp.maximum(group - 1, 0)))
            fresh = product(group)
            total = jnp.where(new, fresh, total + fresh)
            store(pl.ds(pl.multiple_of(target * TILE, TILE), TILE), total)
        return total

    turns = (groups + length - 1) // length
    lax.fori_loop(0, turns, turn, jnp.zeros((TILE, TILE), jnp.float32))


def forward_kernel(pieces, lists, wave, capacity, list_ref, hold_ref, *refs):
    first = wave == 0
    x_refs, refs = refs[:pieces], refs[pieces:]
    codes = lists * capacity * FORWARD_WIDTH
    ends = codes + lists * capacity
    copies = []
    if first:
        tiles_ref = hold_ref
        total_ref, x_ref, hold_ref, sems = refs
        slots = [list_ref[ends + lists + 1 + item] for item in FORWARD_WAVES[0]]
        copies = tile_copies(slots, tiles_ref, hold_ref, sems)
        for copy in copies:
            copy.start()
        total_ref[...] = jnp.zeros_like(total_ref)
    else:
        before_ref, out_refs, (total_ref, x_ref) = refs[0], refs[1:-2], refs[-2:]
        total_ref[...] = before_ref[...].astype(jnp.bfloat16)
    start = 0
    for piece_ref in x_refs:
        x_ref[start : start + piece_ref.shape[0], :] = piece_ref[...]
        start += piece_ref.shape[0]
    x_ref[start:, :] = jnp.zeros((TILE, TILE), jnp.bfloat16)
    for copy in copies:
        copy.wait()

    def product(group):
        begin = (wave * capacity + group) * FORWARD_WIDTH
        codes = [list_ref[begin + item] for item in range(FORWARD_WIDTH)]
        left = jnp.concatenate([hold_ref[code // CODE] for code in codes], axis=1)
        starts = [pl.multiple_of(code % CODE * TILE, TILE) for code in codes]
        right = jnp.concatenate([x_ref[pl.ds(start, TILE), :] for start in starts], axis=0)
        return jnp.dot(left, right, preferred_element_type=jnp.float32)

    def store(span, total):
        if first:
            total_ref[span, :] = total
        else:
            total_ref[span, :] = (total + before_ref[span, :]).astype(jnp.bfloat16)

    group_turns(
        list_ref[ends + wave],
        FORWARD_TURN,
        lambda group: list_ref[codes + wave * capacity + group],
        store,
        product,
    )
    if not first:
        reps = len(out_refs)
        own = out_refs[0].shape[0]
        here = list_ref[ends + lists]
        for shift, out_ref in enumerate(out_refs):
            start = pl.multiple_of((here + shift) % reps * own, own)
            out_ref[...] = total_ref[pl.ds(start, own), :]


def estimate(tiles):
    return pl.CostEstimate(
        flops=8 * tiles * TILE**3, bytes_accessed=tiles * TILE * TILE * 2, transcendentals=0
    )


def forward_product(rows, lists, wave, packed, capacity, tiles, xs, before, reps):
    first = wave == 0
    total_shape = (rows + TILE, TILE)
    x_rows = sum(x.shape[0] for x in xs)
    x_scratch = pltpu.VMEM((x_rows + TILE, TILE), jnp.bfloat16)
    in_specs = [whole()] * (1 + len(xs))
    if first:
        operands = [tiles, *xs]
        in_specs[0] = pl.BlockSpec(memory_space=pltpu.HBM)
        out_shape = jax.ShapeDtypeStruct(total_shape, jnp.float32)
        out_specs = whole()
        count = len(FORWARD_WAVES[0])
        held = (tiles.shape[0] // (lists * count) * count, TILE, TILE)
        scratch = [
            x_scratch,
            pltpu.VMEM(held, jnp.bfloat16),
            pltpu.SemaphoreType.DMA((count * PARTS,)),
        ]
    else:
        operands = [tiles, *xs, before]
        in_specs.append(whole())
        out_shape = [jax.ShapeDtypeStruct((rows // reps, TILE), jnp.bfloat16)] * reps
        out_specs = [whole()] * reps
        scratch = [pltpu.VMEM(total_shape, jnp.bfloat16), x_scratch]
    return pl.pallas_call(
        functools.partial(forward_kernel, len(xs), lists, wave, capacity),
        out_shape=out_shape,
        grid_spec=pltpu.PrefetchScalarGridSpec(
            num_scalar_prefetch=1,
            grid=(),
            in_specs=in_specs,
            out_specs=out_specs,
            scratch_shapes=scratch,
        ),
        compiler_params=params(STREAM_LIMIT if first else VMEM_LIMIT),
        cost_estimate=estimate(x_rows // rows * 80),
    )(packed, *operands)


def dense_kernel(*refs):
    part_refs, (weight_ref, upstream_ref, act_ref, pay_ref) = refs[:-4], refs[-4:]
    rows = upstream_ref.shape[0]
    total = part_refs[0][...].astype(jnp.float32)
    for part_ref in part_refs[1:]:
        total = total + part_ref[...].astype(jnp.float32)
    aggregated = total.astype(jnp.bfloat16)
    weight = weight_ref[...]
    pre = jnp.dot(aggregated, weight, preferred_element_type=jnp.float32)
    gate = jax.nn.sigmoid(pre)
    act_ref[...] = (pre * gate).astype(jnp.bfloat16)
    grad_pre = (
        upstream_ref[...].astype(jnp.float32) * gate * (1.0 + pre * (1.0 - gate))
    ).astype(jnp.bfloat16)
    back = lax.dot_general(
        weight, grad_pre, (((1,), (1,)), ((), ())), preferred_element_type=jnp.float32
    ).astype(jnp.bfloat16)
    for block in range(rows // TILE):
        pay_ref[block * TILE : (block + 1) * TILE, :] = back[:, block * TILE : (block + 1) * TILE]
    local = lax.dot_general(
        aggregated, grad_pre, (((0,), (0,)), ((), ())), preferred_element_type=jnp.float32
    ).astype(jnp.bfloat16)
    for half in range(weight.shape[1] // TILE):
        pay_ref[rows + half * TILE : rows + (half + 1) * TILE, :] = local[
            :, half * TILE : (half + 1) * TILE
        ]


def dense_layer(parts, weight, upstream):
    rows, hidden = upstream.shape
    pay_rows = rows + hidden // TILE * weight.shape[0]
    return pl.pallas_call(
        dense_kernel,
        out_shape=(
            jax.ShapeDtypeStruct((rows, hidden), jnp.bfloat16),
            jax.ShapeDtypeStruct((pay_rows, TILE), jnp.bfloat16),
        ),
        in_specs=[whole()] * (len(parts) + 2),
        out_specs=(whole(), whole()),
        compiler_params=params(),
    )(*parts, weight, upstream)


def backward_kernel(sizes, rows, lists, first, capacity, list_ref, hold_ref, *refs):
    pay_refs, out_refs = refs[: -2 - len(sizes)], refs[-2 - len(sizes) : -2]
    count = sum(sizes)
    spots_of = [(number, item) for number, size in enumerate(sizes) for item in range(size)]
    total_ref, back_ref = refs[-2:]
    reps = len(pay_refs)
    own = rows // reps
    per_slot = hold_ref.shape[0] // count
    codes = lists * capacity * BACKWARD_WIDTH
    ends = codes + lists * capacity
    place = ends + lists
    here = list_ref[place]
    for shift, pay_ref in enumerate(pay_refs):
        start = pl.multiple_of((here + reps - shift) % reps * own, own)
        back_ref[pl.ds(start, own), :] = pay_ref[:own, :]
    back_ref[rows:, :] = jnp.zeros((TILE, TILE), jnp.bfloat16)
    total_ref[...] = jnp.zeros_like(total_ref)
    if out_refs[0].shape[0] > sizes[0] * rows:
        ride = pay_refs[0][own:, :].astype(jnp.float32)
        for pay_ref in pay_refs[1:]:
            ride = ride + pay_ref[own:, :].astype(jnp.float32)
        out_refs[0][sizes[0] * rows :, :] = ride.astype(jnp.bfloat16)
    for number in range(0, count, PAIR):
        listed = first + number // PAIR

        def product(group, listed=listed, number=number):
            begin = (listed * capacity + group) * BACKWARD_WIDTH
            items = [list_ref[begin + item] for item in range(BACKWARD_WIDTH)]
            starts = [pl.multiple_of(code % CODE * TILE, TILE) for code in items]
            left = jnp.concatenate([back_ref[pl.ds(start, TILE), :] for start in starts], axis=1)
            right = jnp.concatenate(
                [hold_ref[number * per_slot + code // CODE] for code in items], axis=0
            )
            return jnp.dot(left, right, preferred_element_type=jnp.float32)

        def target_of(group, listed=listed):
            return list_ref[codes + listed * capacity + group]

        def store(span, total):
            total_ref[span, :] = total.astype(jnp.bfloat16)

        group_turns(list_ref[ends + listed], BACKWARD_TURN, target_of, store, product)
        for item in range(PAIR):
            target, spot = spots_of[number + item]
            out_refs[target][spot * rows : (spot + 1) * rows, :] = total_ref[
                item * rows : (item + 1) * rows, :
            ]
        if number + PAIR < count:
            total_ref[...] = jnp.zeros_like(total_ref)


def backward_product(sizes, rows, lists, first, packed, capacity, held, pays):
    out_rows = [size * rows for size in sizes]
    if first == 0:
        out_rows[0] += pays[0].shape[0] - rows // len(pays)
    return pl.pallas_call(
        functools.partial(backward_kernel, sizes, rows, lists, first, capacity),
        out_shape=[jax.ShapeDtypeStruct((size, TILE), jnp.bfloat16) for size in out_rows],
        grid_spec=pltpu.PrefetchScalarGridSpec(
            num_scalar_prefetch=1,
            grid=(),
            in_specs=[whole()] * (1 + len(pays)),
            out_specs=[whole()] * len(sizes),
            scratch_shapes=[
                pltpu.VMEM((PAIR * rows + TILE, TILE), jnp.bfloat16),
                pltpu.VMEM((rows + TILE, TILE), jnp.bfloat16),
            ],
        ),
        compiler_params=params(),
        cost_estimate=estimate(held.shape[0]),
    )(packed, held, *pays)


def restore_kernel(place_ref, order_ref, home_ref, *refs):
    out_refs, part_ref = refs[:-1], refs[-1]
    rows = order_ref.shape[1]
    reps = len(out_refs)
    own = rows // reps
    for block in range(rows // TILE):
        span = slice(block * TILE, (block + 1) * TILE)
        part_ref[span, :] = home_ref[span, :].astype(jnp.float32).T.astype(jnp.bfloat16)
    order = order_ref[...]
    part = part_ref[...]
    for shift, out_ref in enumerate(out_refs):
        start = (place_ref[0] + shift) % reps * own
        level = lax.broadcasted_iota(jnp.int32, (own, rows), 0) + start
        pick = (jnp.broadcast_to(order, (own, rows)) == level).astype(jnp.float32)
        out_ref[:own, :] = jnp.dot(
            pick.astype(jnp.bfloat16), part, preferred_element_type=jnp.float32
        ).astype(jnp.bfloat16)
        out_ref[own:, :] = home_ref[rows:, :]


def restore(place, order, home, reps):
    rows = order.shape[1]
    out_rows = rows // reps + home.shape[0] - rows
    out_shape = jax.ShapeDtypeStruct((out_rows, TILE), jnp.bfloat16)
    return pl.pallas_call(
        restore_kernel,
        out_shape=[out_shape] * reps,
        grid_spec=pltpu.PrefetchScalarGridSpec(
            num_scalar_prefetch=1,
            grid=(),
            in_specs=[whole()] * 2,
            out_specs=[whole()] * reps,
            scratch_shapes=[pltpu.VMEM((rows, TILE), jnp.bfloat16)],
        ),
        compiler_params=params(),
    )(place, order, home)


def added(*values):
    return sum(value.astype(jnp.float32) for value in values).astype(jnp.bfloat16)


def per_device(features, node_order, adj_values, adj_rows, adj_cols, tile_count, weight, upstream):
    reps = lax.axis_size("rep")
    slices = lax.axis_size("blk")
    steps = slices // reps
    rows_dev = features.shape[0]
    blocks = rows_dev // TILE
    both = ("blk", "rep")
    row_ids, col_ids, counts = adj_rows[0, 0], adj_cols[0, 0], tile_count[0, 0]
    per_slot = row_ids.shape[1]
    tiles = adj_values.reshape((-1, TILE, TILE))
    own_rep = lax.axis_index("rep").astype(jnp.int32).reshape(1)

    here = lax.axis_index("blk") * reps + lax.axis_index("rep")
    slots = lax.dynamic_index_in_dim(jnp.asarray(slot_table()), here, 0, keepdims=False)
    place = jnp.concatenate([own_rep, slots])
    home_rep = lax.dynamic_index_in_dim(jnp.asarray(rep_table()), here, 0, keepdims=False)
    half = rows_dev // 2

    def moved(value, listed):
        return lax.ppermute(value, both, listed)

    def up(value):
        return moved(value, ring_pairs(1))

    def down(value):
        return moved(value, ring_pairs(-1))

    def swapped(value):
        return moved(value, partner_pairs())

    def to_reps(values):
        received = [values[0]]
        for shift in range(1, reps):
            along = [(rep, (rep + shift) % reps) for rep in range(reps)]
            received.append(lax.ppermute(values[shift], "rep", along))
        return received

    blocked = order_rows(node_order, features)
    near = moved(blocked, fetch_pairs())
    near_order = moved(node_order, fetch_pairs())
    alive = jnp.arange(per_slot, dtype=jnp.int32)[None, :] < counts[:, None]
    cells = jnp.take(jnp.where(alive, row_ids * CODE + col_ids, -1), slots, axis=0)

    def split(cells, items):
        chosen = jnp.concatenate([cells[item : item + 1] for item in items])
        return chosen >= 0, chosen // CODE, chosen % CODE

    waves = len(FORWARD_WAVES)
    alive, rows_of, cols_of = split(cells, sum(FORWARD_WAVES, ()))
    offsets = jnp.arange(steps, dtype=jnp.int32)[:, None] % (steps // waves) * blocks
    forward_list, forward_capacity = tile_lists(
        jnp.where(alive, rows_of, blocks).reshape(waves, -1),
        (cols_of + offsets).reshape(waves, -1),
        blocks,
        steps // waves * blocks,
        FORWARD_WIDTH,
        FORWARD_TURN,
    )
    forward_list = jnp.concatenate([forward_list, place])
    late_cells, near = lax.optimization_barrier((cells, near))
    lists = steps // PAIR
    alive, rows_of, cols_of = split(late_cells, sum(BACKWARD_WAVES, ()))
    offsets = jnp.arange(steps, dtype=jnp.int32)[:, None] % PAIR * blocks
    packed, capacity = tile_lists(
        jnp.where(alive, cols_of + offsets, PAIR * blocks).reshape(lists, -1),
        rows_of.reshape(lists, -1),
        PAIR * blocks,
        blocks,
        BACKWARD_WIDTH,
        BACKWARD_TURN,
    )
    packed = jnp.concatenate([packed, own_rep])
    above, below = down(near), up(near)
    ready, packed = lax.optimization_barrier((near, packed))
    far = swapped(ready)
    above, below, far, forward_list, packed, near_order = lax.optimization_barrier(
        (above, below, far, forward_list, packed, near_order)
    )
    middle = [down(above[:half]), up(below[half:])]
    known, far = lax.optimization_barrier((place, far))
    held = hold(FORWARD_WAVES[1], known, tiles, per_slot)
    xs = [near, above, below, *middle]
    total = forward_product(
        rows_dev, waves, 0, forward_list, forward_capacity, tiles, xs, None, reps
    )
    xs = [far, swapped(above), swapped(below), *[swapped(value) for value in middle]]
    total = list(
        forward_product(
            rows_dev, waves, 1, forward_list, forward_capacity, held, xs, total, reps
        )
    )
    known, total[0] = lax.optimization_barrier((place, total[0]))
    shared = to_reps(total)
    holds = [hold(BACKWARD_WAVES[0], known, tiles, per_slot)]
    shared[1], holds[0] = lax.optimization_barrier((shared[1], holds[0]))
    activations, pay = dense_layer(shared, weight, upstream)
    known, pay = lax.optimization_barrier((place, pay))
    pays = to_reps([pay] * reps)
    holds.append(hold(BACKWARD_WAVES[1], known, tiles, per_slot))
    packed, holds = lax.optimization_barrier((packed, holds))

    def products(wave, packed):
        sizes = BACKWARD_OUTPUTS[wave]
        first = wave * sum(sizes) // PAIR
        return list(
            backward_product(sizes, rows_dev, lists, first, packed, capacity, holds[wave], pays)
        )

    others = products(0, packed)
    packed, others[2] = lax.optimization_barrier((packed, others[2]))
    returned = swapped(others[0])
    sides = swapped(others[1])
    last = swapped(others[2])
    mine = products(1, packed)
    two = added(mine[2], returned[:rows_dev])
    ride = added(others[0][rows_dev:], returned[rows_dev:])
    from_below, from_above = lax.optimization_barrier(
        (up(jnp.concatenate([two[:half], ride])), down(jnp.concatenate([two[half:], ride])))
    )
    one = jnp.concatenate(
        [
            added(mine[1][:half], sides[:half], from_below[:half]),
            added(mine[1][half:], sides[half:rows_dev]),
            from_below[half:],
        ]
    )
    three = jnp.concatenate(
        [
            added(mine[3][:half], sides[rows_dev : rows_dev + half]),
            added(mine[3][half:], sides[rows_dev + half :], from_above[:half]),
        ]
    )
    below_sum, above_sum = up(one), down(three)
    ended = jnp.concatenate(
        [
            added(mine[0], last, below_sum[:rows_dev], above_sum),
            added(ride, from_below[half:], from_above[half:], below_sum[rows_dev:]),
        ]
    )
    quarters = restore(home_rep, near_order, ended, reps)
    terms = [moved(value, quarter_pairs(shift)) for shift, value in enumerate(quarters)]
    own = rows_dev // reps
    grad_features = added(*[term[:own] for term in terms])
    grad_weight = sum(term[own:].astype(jnp.float32) for term in terms)
    stacked = grad_weight.reshape(weight.shape[1] // TILE, weight.shape[0], TILE)
    grad_weight = jnp.concatenate([stacked[half] for half in range(stacked.shape[0])], axis=1)
    return (activations, grad_weight, grad_features)


def solution(mesh):
    placed = (
        P("blk", None),
        P("blk", None),
        P("blk", "rep", None, None, None, None),
        P("blk", "rep", None, None),
        P("blk", "rep", None, None),
        P("blk", "rep", None),
        P(),
        P(("blk", "rep"), None),
    )
    return jax.shard_map(
        per_device,
        mesh=mesh,
        in_specs=placed,
        out_specs=(P(("blk", "rep"), None), P(), P(("blk", "rep"), None)),
        check_vma=False,
    )
```

```python
import functools

import jax
import jax.numpy as jnp
import numpy as np
from jax import lax
from jax.experimental import pallas as pl
from jax.experimental.pallas import tpu as pltpu
from jax.sharding import PartitionSpec as P

TILE = 128
FORWARD_TURN = 4
BACKWARD_TURN = 16
FORWARD_WIDTH = 8
BACKWARD_WIDTH = 2
FORWARD_WAVES = ((0, 1, 3, 2), (4, 5, 7, 6))
BACKWARD_WAVES = ((6, 5, 7, 4), (0, 1, 2, 3))
BACKWARD_OUTPUTS = ((1, 2, 1), (1, 1, 1, 1))
PAIR = 2
PARTS = 4
CODE = 256
VMEM_LIMIT = 12 * 1024 * 1024
HOLD_LIMIT = 32 * 1024 * 1024
STREAM_LIMIT = 40 * 1024 * 1024


def spots():
    return [(x, y, z, c) for x in range(4) for y in range(4) for z in range(4) for c in range(2)]


def coords(x, y, z, c):
    return 8 * y + 2 * z + x % 2, x // 2 * 2 + c


def device(x, y, z, c):
    blk, rep = coords(x % 4, y % 4, z % 4, c)
    return 4 * blk + rep


def levels(x, y, z, c):
    kind = sum(coords(x, y, z, c)) % 4
    level = z if kind // 2 == z % 2 else z + 1
    return kind % 2, (level + 2 * c) % 4, (level + 2 - 2 * c) % 4


def slot_table():
    table = np.zeros((128, 8), np.int32)
    for spot in spots():
        low, near, far = levels(*spot)
        base = sum(coords(*spot))
        for item in range(8):
            row = (spot[1] + item) % 4
            wanted = 8 * row + 2 * (near if item < 4 else far) + low
            table[device(*spot), item] = (wanted - base) % 32 // 4
    return table


def fetch_pairs():
    listed = []
    for x, y, z, c in spots():
        near = levels(x, y, z, c)[1]
        listed.append((device(x - c, y, near, c), device(x, y, z, c)))
    return listed


def fetched_rep(x, y, z, c):
    return coords((x - c) % 4, y, z, c)[1]


def quarter_pairs(shift):
    listed = []
    for x, y, z, c in spots():
        near = levels(x, y, z, c)[1]
        blk = device(x - c, y, near, c) // 4
        listed.append((device(x, y, z, c), 4 * blk + (fetched_rep(x, y, z, c) + shift) % 4))
    return listed


def rep_table():
    table = np.zeros((128, 1), np.int32)
    for spot in spots():
        table[device(*spot), 0] = fetched_rep(*spot)
    return table


def partner_pairs():
    return [(device(x, y, z, c), device(x + 2 * c - 1, y, z, 1 - c)) for x, y, z, c in spots()]


def ring_pairs(step):
    return [(device(x, y, z, c), device(x, y + step, z, c)) for x, y, z, c in spots()]


def params(limit=VMEM_LIMIT):
    return pltpu.CompilerParams(vmem_limit_bytes=limit)


def whole():
    return pl.BlockSpec(memory_space=pltpu.VMEM)


def order_kernel(order_ref, feat_ref, out_ref):
    rows = feat_ref.shape[0]
    step = 512
    feats = feat_ref[...]
    for start in range(0, rows, step):
        parts = []
        for inner in range(start, start + step, TILE):
            line = order_ref[0:1, inner : inner + TILE]
            parts.append(jnp.broadcast_to(line, (TILE, TILE)).T)
        column = jnp.concatenate(parts, axis=0)
        pieces = []
        for col in range(0, rows, TILE):
            level = lax.broadcasted_iota(jnp.int32, (step, TILE), 1) + col
            pieces.append((column == level).astype(jnp.float32).astype(jnp.bfloat16))
        pick = jnp.concatenate(pieces, axis=1)
        out_ref[start : start + step, :] = jnp.dot(
            pick, feats, preferred_element_type=jnp.float32
        ).astype(jnp.bfloat16)


def order_rows(order, features):
    return pl.pallas_call(
        order_kernel,
        out_shape=jax.ShapeDtypeStruct(features.shape, jnp.bfloat16),
        in_specs=[whole(), whole()],
        out_specs=whole(),
        compiler_params=params(),
    )(order, features)


def tile_copies(slots, tiles_ref, out_ref, sems):
    per_slot = out_ref.shape[0] // len(slots)
    part = per_slot // PARTS
    copies = []
    for number, slot in enumerate(slots):
        for piece in range(PARTS):
            target = number * per_slot + piece * part
            copies.append(
                pltpu.make_async_copy(
                    tiles_ref.at[pl.ds(slot * per_slot + piece * part, part)],
                    out_ref.at[pl.ds(target, part)],
                    sems.at[number * PARTS + piece],
                )
            )
    return copies


def hold_kernel(items, place_ref, tiles_ref, out_ref, sems):
    slots = [place_ref[1 + item] for item in items]
    copies = tile_copies(slots, tiles_ref, out_ref, sems)
    for copy in copies:
        copy.start()
    for copy in copies:
        copy.wait()


def hold(items, place, tiles, per_slot):
    size = len(items) * per_slot
    return pl.pallas_call(
        functools.partial(hold_kernel, items),
        out_shape=jax.ShapeDtypeStruct((size, TILE, TILE), tiles.dtype),
        grid_spec=pltpu.PrefetchScalarGridSpec(
            num_scalar_prefetch=1,
            grid=(),
            in_specs=[pl.BlockSpec(memory_space=pltpu.HBM)],
            out_specs=whole(),
            scratch_shapes=[pltpu.SemaphoreType.DMA((len(items) * PARTS,))],
        ),
        compiler_params=params(HOLD_LIMIT),
        cost_estimate=pl.CostEstimate(
            flops=0, bytes_accessed=4 * size * TILE * TILE, transcendentals=0
        ),
    )(place, tiles)


def tile_lists(key, source, target_count, zero, width, turn):
    lists, size = key.shape
    capacity = (size + target_count * (width - 1)) // width
    capacity = -(-capacity // turn) * turn
    ids = jnp.arange(size, dtype=jnp.int32)
    levels = jnp.arange(target_count, dtype=jnp.int32)
    earlier = (key[:, None, :] == key[:, :, None]) & (ids[None, :] < ids[:, None])
    rank = jnp.sum(earlier.astype(jnp.int32), axis=2)
    held = jnp.sum((key[:, None, :] == levels[:, None]).astype(jnp.int32), axis=2)
    needed = (held + width - 1) // width
    upto = levels[None, :] <= levels[:, None]
    ends = jnp.sum(jnp.where(upto, needed[:, None, :], 0), axis=2)
    base = jnp.sum(jnp.where(levels < key[:, :, None], needed[:, None, :], 0), axis=2)
    place = jnp.where(key < target_count, base * width + rank, -1)
    cells = jnp.arange(capacity * width, dtype=jnp.int32)
    hit = (place[:, None, :] == cells[:, None]).astype(jnp.int32)
    tile = jnp.sum(hit * ids, axis=2)
    origin = zero + jnp.sum(hit * (source - zero)[:, None, :], axis=2)
    groups = jnp.arange(capacity, dtype=jnp.int32)
    target = jnp.sum((ends[:, None, :] <= groups[:, None]).astype(jnp.int32), axis=2)
    code = tile * CODE + origin
    packed = jnp.concatenate([code.reshape(-1), target.reshape(-1), jnp.max(ends, axis=1)])
    return packed, capacity


def group_turns(groups, length, target_of, store, product):
    def turn(index, total):
        for lane in range(length):
            group = index * length + lane
            target = target_of(group)
            new = (group == 0) | (target != target_of(jnp.maximum(group - 1, 0)))
            fresh = product(group)
            total = jnp.where(new, fresh, total + fresh)
            store(pl.ds(pl.multiple_of(target * TILE, TILE), TILE), total)
        return total

    turns = (groups + length - 1) // length
    lax.fori_loop(0, turns, turn, jnp.zeros((TILE, TILE), jnp.float32))


def forward_kernel(pieces, lists, wave, capacity, list_ref, hold_ref, *refs):
    first = wave == 0
    x_refs, refs = refs[:pieces], refs[pieces:]
    codes = lists * capacity * FORWARD_WIDTH
    ends = codes + lists * capacity
    copies = []
    if first:
        tiles_ref = hold_ref
        total_ref, x_ref, hold_ref, sems = refs
        slots = [list_ref[ends + lists + 1 + item] for item in FORWARD_WAVES[0]]
        copies = tile_copies(slots, tiles_ref, hold_ref, sems)
        for copy in copies:
            copy.start()
        total_ref[...] = jnp.zeros_like(total_ref)
    else:
        before_ref, out_refs, (total_ref, x_ref) = refs[0], refs[1:-2], refs[-2:]
        total_ref[...] = before_ref[...].astype(jnp.bfloat16)
    start = 0
    for piece_ref in x_refs:
        x_ref[start : start + piece_ref.shape[0], :] = piece_ref[...]
        start += piece_ref.shape[0]
    x_ref[start:, :] = jnp.zeros((TILE, TILE), jnp.bfloat16)
    for copy in copies:
        copy.wait()

    def product(group):
        begin = (wave * capacity + group) * FORWARD_WIDTH
        codes = [list_ref[begin + item] for item in range(FORWARD_WIDTH)]
        left = jnp.concatenate([hold_ref[code // CODE] for code in codes], axis=1)
        starts = [pl.multiple_of(code % CODE * TILE, TILE) for code in codes]
        right = jnp.concatenate([x_ref[pl.ds(start, TILE), :] for start in starts], axis=0)
        return jnp.dot(left, right, preferred_element_type=jnp.float32)

    def store(span, total):
        if first:
            total_ref[span, :] = total
        else:
            total_ref[span, :] = (total + before_ref[span, :]).astype(jnp.bfloat16)

    group_turns(
        list_ref[ends + wave],
        FORWARD_TURN,
        lambda group: list_ref[codes + wave * capacity + group],
        store,
        product,
    )
    if not first:
        reps = len(out_refs)
        own = out_refs[0].shape[0]
        here = list_ref[ends + lists]
        for shift, out_ref in enumerate(out_refs):
            start = pl.multiple_of((here + shift) % reps * own, own)
            out_ref[...] = total_ref[pl.ds(start, own), :]


def estimate(tiles):
    return pl.CostEstimate(
        flops=8 * tiles * TILE**3, bytes_accessed=tiles * TILE * TILE * 2, transcendentals=0
    )


def forward_product(rows, lists, wave, packed, capacity, tiles, xs, before, reps):
    first = wave == 0
    total_shape = (rows + TILE, TILE)
    x_rows = sum(x.shape[0] for x in xs)
    x_scratch = pltpu.VMEM((x_rows + TILE, TILE), jnp.bfloat16)
    in_specs = [whole()] * (1 + len(xs))
    if first:
        operands = [tiles, *xs]
        in_specs[0] = pl.BlockSpec(memory_space=pltpu.HBM)
        out_shape = jax.ShapeDtypeStruct(total_shape, jnp.float32)
        out_specs = whole()
        count = len(FORWARD_WAVES[0])
        held = (tiles.shape[0] // (lists * count) * count, TILE, TILE)
        scratch = [
            x_scratch,
            pltpu.VMEM(held, jnp.bfloat16),
            pltpu.SemaphoreType.DMA((count * PARTS,)),
        ]
    else:
        operands = [tiles, *xs, before]
        in_specs.append(whole())
        out_shape = [jax.ShapeDtypeStruct((rows // reps, TILE), jnp.bfloat16)] * reps
        out_specs = [whole()] * reps
        scratch = [pltpu.VMEM(total_shape, jnp.bfloat16), x_scratch]
    return pl.pallas_call(
        functools.partial(forward_kernel, len(xs), lists, wave, capacity),
        out_shape=out_shape,
        grid_spec=pltpu.PrefetchScalarGridSpec(
            num_scalar_prefetch=1,
            grid=(),
            in_specs=in_specs,
            out_specs=out_specs,
            scratch_shapes=scratch,
        ),
        compiler_params=params(STREAM_LIMIT if first else VMEM_LIMIT),
        cost_estimate=estimate(x_rows // rows * 80),
    )(packed, *operands)


def dense_kernel(*refs):
    part_refs, (weight_ref, upstream_ref, act_ref, pay_ref) = refs[:-4], refs[-4:]
    rows = upstream_ref.shape[0]
    total = part_refs[0][...].astype(jnp.float32)
    for part_ref in part_refs[1:]:
        total = total + part_ref[...].astype(jnp.float32)
    aggregated = total.astype(jnp.bfloat16)
    weight = weight_ref[...]
    pre = jnp.dot(aggregated, weight, preferred_element_type=jnp.float32)
    gate = jax.nn.sigmoid(pre)
    act_ref[...] = (pre * gate).astype(jnp.bfloat16)
    grad_pre = (
        upstream_ref[...].astype(jnp.float32) * gate * (1.0 + pre * (1.0 - gate))
    ).astype(jnp.bfloat16)
    back = lax.dot_general(
        weight, grad_pre, (((1,), (1,)), ((), ())), preferred_element_type=jnp.float32
    ).astype(jnp.bfloat16)
    for block in range(rows // TILE):
        pay_ref[block * TILE : (block + 1) * TILE, :] = back[:, block * TILE : (block + 1) * TILE]
    local = lax.dot_general(
        aggregated, grad_pre, (((0,), (0,)), ((), ())), preferred_element_type=jnp.float32
    ).astype(jnp.bfloat16)
    for half in range(weight.shape[1] // TILE):
        pay_ref[rows + half * TILE : rows + (half + 1) * TILE, :] = local[
            :, half * TILE : (half + 1) * TILE
        ]


def dense_layer(parts, weight, upstream):
    rows, hidden = upstream.shape
    pay_rows = rows + hidden // TILE * weight.shape[0]
    return pl.pallas_call(
        dense_kernel,
        out_shape=(
            jax.ShapeDtypeStruct((rows, hidden), jnp.bfloat16),
            jax.ShapeDtypeStruct((pay_rows, TILE), jnp.bfloat16),
        ),
        in_specs=[whole()] * (len(parts) + 2),
        out_specs=(whole(), whole()),
        compiler_params=params(),
    )(*parts, weight, upstream)


def backward_kernel(sizes, rows, lists, first, capacity, list_ref, hold_ref, *refs):
    pay_refs, out_refs = refs[: -2 - len(sizes)], refs[-2 - len(sizes) : -2]
    count = sum(sizes)
    spots_of = [(number, item) for number, size in enumerate(sizes) for item in range(size)]
    total_ref, back_ref = refs[-2:]
    reps = len(pay_refs)
    own = rows // reps
    per_slot = hold_ref.shape[0] // count
    codes = lists * capacity * BACKWARD_WIDTH
    ends = codes + lists * capacity
    place = ends + lists
    here = list_ref[place]
    for shift, pay_ref in enumerate(pay_refs):
        start = pl.multiple_of((here + reps - shift) % reps * own, own)
        back_ref[pl.ds(start, own), :] = pay_ref[:own, :]
    back_ref[rows:, :] = jnp.zeros((TILE, TILE), jnp.bfloat16)
    total_ref[...] = jnp.zeros_like(total_ref)
    if out_refs[0].shape[0] > sizes[0] * rows:
        ride = pay_refs[0][own:, :].astype(jnp.float32)
        for pay_ref in pay_refs[1:]:
            ride = ride + pay_ref[own:, :].astype(jnp.float32)
        out_refs[0][sizes[0] * rows :, :] = ride.astype(jnp.bfloat16)
    for number in range(0, count, PAIR):
        listed = first + number // PAIR

        def product(group, listed=listed, number=number):
            begin = (listed * capacity + group) * BACKWARD_WIDTH
            items = [list_ref[begin + item] for item in range(BACKWARD_WIDTH)]
            starts = [pl.multiple_of(code % CODE * TILE, TILE) for code in items]
            left = jnp.concatenate([back_ref[pl.ds(start, TILE), :] for start in starts], axis=1)
            right = jnp.concatenate(
                [hold_ref[number * per_slot + code // CODE] for code in items], axis=0
            )
            return jnp.dot(left, right, preferred_element_type=jnp.float32)

        def target_of(group, listed=listed):
            return list_ref[codes + listed * capacity + group]

        def store(span, total):
            total_ref[span, :] = total.astype(jnp.bfloat16)

        group_turns(list_ref[ends + listed], BACKWARD_TURN, target_of, store, product)
        for item in range(PAIR):
            target, spot = spots_of[number + item]
            out_refs[target][spot * rows : (spot + 1) * rows, :] = total_ref[
                item * rows : (item + 1) * rows, :
            ]
        if number + PAIR < count:
            total_ref[...] = jnp.zeros_like(total_ref)


def backward_product(sizes, rows, lists, first, packed, capacity, held, pays):
    out_rows = [size * rows for size in sizes]
    if first == 0:
        out_rows[0] += pays[0].shape[0] - rows // len(pays)
    return pl.pallas_call(
        functools.partial(backward_kernel, sizes, rows, lists, first, capacity),
        out_shape=[jax.ShapeDtypeStruct((size, TILE), jnp.bfloat16) for size in out_rows],
        grid_spec=pltpu.PrefetchScalarGridSpec(
            num_scalar_prefetch=1,
            grid=(),
            in_specs=[whole()] * (1 + len(pays)),
            out_specs=[whole()] * len(sizes),
            scratch_shapes=[
                pltpu.VMEM((PAIR * rows + TILE, TILE), jnp.bfloat16),
                pltpu.VMEM((rows + TILE, TILE), jnp.bfloat16),
            ],
        ),
        compiler_params=params(),
        cost_estimate=estimate(held.shape[0]),
    )(packed, held, *pays)


def restore_kernel(place_ref, order_ref, home_ref, *refs):
    out_refs, part_ref = refs[:-1], refs[-1]
    rows = order_ref.shape[1]
    reps = len(out_refs)
    own = rows // reps
    for block in range(rows // TILE):
        span = slice(block * TILE, (block + 1) * TILE)
        part_ref[span, :] = home_ref[span, :].astype(jnp.float32).T.astype(jnp.bfloat16)
    order = order_ref[...]
    part = part_ref[...]
    for shift, out_ref in enumerate(out_refs):
        start = (place_ref[0] + shift) % reps * own
        level = lax.broadcasted_iota(jnp.int32, (own, rows), 0) + start
        pick = (jnp.broadcast_to(order, (own, rows)) == level).astype(jnp.float32)
        out_ref[:own, :] = jnp.dot(
            pick.astype(jnp.bfloat16), part, preferred_element_type=jnp.float32
        ).astype(jnp.bfloat16)
        out_ref[own:, :] = home_ref[rows:, :]


def restore(place, order, home, reps):
    rows = order.shape[1]
    out_rows = rows // reps + home.shape[0] - rows
    out_shape = jax.ShapeDtypeStruct((out_rows, TILE), jnp.bfloat16)
    return pl.pallas_call(
        restore_kernel,
        out_shape=[out_shape] * reps,
        grid_spec=pltpu.PrefetchScalarGridSpec(
            num_scalar_prefetch=1,
            grid=(),
            in_specs=[whole()] * 2,
            out_specs=[whole()] * reps,
            scratch_shapes=[pltpu.VMEM((rows, TILE), jnp.bfloat16)],
        ),
        compiler_params=params(),
    )(place, order, home)


def added(*values):
    return sum(value.astype(jnp.float32) for value in values).astype(jnp.bfloat16)


def per_device(features, node_order, adj_values, adj_rows, adj_cols, tile_count, weight, upstream):
    reps = lax.axis_size("rep")
    slices = lax.axis_size("blk")
    steps = slices // reps
    rows_dev = features.shape[0]
    blocks = rows_dev // TILE
    both = ("blk", "rep")
    row_ids, col_ids, counts = adj_rows[0, 0], adj_cols[0, 0], tile_count[0, 0]
    per_slot = row_ids.shape[1]
    tiles = adj_values.reshape((-1, TILE, TILE))
    own_rep = lax.axis_index("rep").astype(jnp.int32).reshape(1)

    here = lax.axis_index("blk") * reps + lax.axis_index("rep")
    slots = lax.dynamic_index_in_dim(jnp.asarray(slot_table()), here, 0, keepdims=False)
    place = jnp.concatenate([own_rep, slots])
    home_rep = lax.dynamic_index_in_dim(jnp.asarray(rep_table()), here, 0, keepdims=False)
    half = rows_dev // 2

    def moved(value, listed):
        return lax.ppermute(value, both, listed)

    def up(value):
        return moved(value, ring_pairs(1))

    def down(value):
        return moved(value, ring_pairs(-1))

    def swapped(value):
        return moved(value, partner_pairs())

    def to_reps(values):
        received = [values[0]]
        for shift in range(1, reps):
            along = [(rep, (rep + shift) % reps) for rep in range(reps)]
            received.append(lax.ppermute(values[shift], "rep", along))
        return received

    blocked = order_rows(node_order, features)
    near = moved(blocked, fetch_pairs())
    later_order, blocked = lax.optimization_barrier((node_order, blocked))
    near_order = moved(later_order, fetch_pairs())
    alive = jnp.arange(per_slot, dtype=jnp.int32)[None, :] < counts[:, None]
    cells = jnp.take(jnp.where(alive, row_ids * CODE + col_ids, -1), slots, axis=0)

    def split(cells, items):
        chosen = jnp.concatenate([cells[item : item + 1] for item in items])
        return chosen >= 0, chosen // CODE, chosen % CODE

    waves = len(FORWARD_WAVES)
    alive, rows_of, cols_of = split(cells, sum(FORWARD_WAVES, ()))
    offsets = jnp.arange(steps, dtype=jnp.int32)[:, None] % (steps // waves) * blocks
    forward_list, forward_capacity = tile_lists(
        jnp.where(alive, rows_of, blocks).reshape(waves, -1),
        (cols_of + offsets).reshape(waves, -1),
        blocks,
        steps // waves * blocks,
        FORWARD_WIDTH,
        FORWARD_TURN,
    )
    forward_list = jnp.concatenate([forward_list, place])
    late_cells, near = lax.optimization_barrier((cells, near))
    lists = steps // PAIR
    alive, rows_of, cols_of = split(late_cells, sum(BACKWARD_WAVES, ()))
    offsets = jnp.arange(steps, dtype=jnp.int32)[:, None] % PAIR * blocks
    packed, capacity = tile_lists(
        jnp.where(alive, cols_of + offsets, PAIR * blocks).reshape(lists, -1),
        rows_of.reshape(lists, -1),
        PAIR * blocks,
        blocks,
        BACKWARD_WIDTH,
        BACKWARD_TURN,
    )
    packed = jnp.concatenate([packed, own_rep])
    above, below = down(near), up(near)
    ready, packed = lax.optimization_barrier((near, packed))
    far = swapped(ready)
    above, below, far, forward_list, packed, near_order = lax.optimization_barrier(
        (above, below, far, forward_list, packed, near_order)
    )
    middle = [down(above[:half]), up(below[half:])]
    known, far = lax.optimization_barrier((place, far))
    held = hold(FORWARD_WAVES[1], known, tiles, per_slot)
    xs = [near, above, below, *middle]
    total = forward_product(
        rows_dev, waves, 0, forward_list, forward_capacity, tiles, xs, None, reps
    )
    xs = [far, swapped(above), swapped(below), *[swapped(value) for value in middle]]
    total = list(
        forward_product(
            rows_dev, waves, 1, forward_list, forward_capacity, held, xs, total, reps
        )
    )
    known, total[0] = lax.optimization_barrier((place, total[0]))
    shared = to_reps(total)
    holds = [hold(BACKWARD_WAVES[0], known, tiles, per_slot)]
    shared[1], holds[0] = lax.optimization_barrier((shared[1], holds[0]))
    activations, pay = dense_layer(shared, weight, upstream)
    known, pay = lax.optimization_barrier((place, pay))
    pays = to_reps([pay] * reps)
    holds.append(hold(BACKWARD_WAVES[1], known, tiles, per_slot))
    packed, holds = lax.optimization_barrier((packed, holds))

    def products(wave, packed):
        sizes = BACKWARD_OUTPUTS[wave]
        first = wave * sum(sizes) // PAIR
        return list(
            backward_product(sizes, rows_dev, lists, first, packed, capacity, holds[wave], pays)
        )

    others = products(0, packed)
    packed, others[2] = lax.optimization_barrier((packed, others[2]))
    returned = swapped(others[0])
    sides = swapped(others[1])
    last = swapped(others[2])
    mine = products(1, packed)
    two = added(mine[2], returned[:rows_dev])
    ride = added(others[0][rows_dev:], returned[rows_dev:])
    from_below, from_above = lax.optimization_barrier(
        (up(jnp.concatenate([two[:half], ride])), down(jnp.concatenate([two[half:], ride])))
    )
    one = jnp.concatenate(
        [
            added(mine[1][:half], sides[:half], from_below[:half]),
            added(mine[1][half:], sides[half:rows_dev]),
            from_below[half:],
        ]
    )
    three = jnp.concatenate(
        [
            added(mine[3][:half], sides[rows_dev : rows_dev + half]),
            added(mine[3][half:], sides[rows_dev + half :], from_above[:half]),
        ]
    )
    below_sum, above_sum = up(one), down(three)
    ended = jnp.concatenate(
        [
            added(mine[0], last, below_sum[:rows_dev], above_sum),
            added(ride, from_below[half:], from_above[half:], below_sum[rows_dev:]),
        ]
    )
    quarters = restore(home_rep, near_order, ended, reps)
    terms = [moved(value, quarter_pairs(shift)) for shift, value in enumerate(quarters)]
    own = rows_dev // reps
    grad_features = added(*[term[:own] for term in terms])
    grad_weight = sum(term[own:].astype(jnp.float32) for term in terms)
    stacked = grad_weight.reshape(weight.shape[1] // TILE, weight.shape[0], TILE)
    grad_weight = jnp.concatenate([stacked[half] for half in range(stacked.shape[0])], axis=1)
    return (activations, grad_weight, grad_features)


def solution(mesh):
    placed = (
        P("blk", None),
        P("blk", None),
        P("blk", "rep", None, None, None, None),
        P("blk", "rep", None, None),
        P("blk", "rep", None, None),
        P("blk", "rep", None),
        P(),
        P(("blk", "rep"), None),
    )
    return jax.shard_map(
        per_device,
        mesh=mesh,
        in_specs=placed,
        out_specs=(P(("blk", "rep"), None), P(), P(("blk", "rep"), None)),
        check_vma=False,
    )
```

```python
import functools

import jax
import jax.numpy as jnp
import numpy as np
from jax import lax
from jax.experimental import pallas as pl
from jax.experimental.pallas import tpu as pltpu
from jax.sharding import PartitionSpec as P

TILE = 128
FORWARD_TURN = 8
BACKWARD_TURN = 16
FORWARD_WIDTH = 4
BACKWARD_WIDTH = 2
FORWARD_WAVES = ((0, 1, 3, 2), (4, 5, 7, 6))
BACKWARD_WAVES = ((6, 5, 7, 4), (0, 1, 2, 3))
BACKWARD_OUTPUTS = ((1, 2, 1), (1, 1, 1, 1))
PAIR = 2
PARTS = 4
CODE = 256
VMEM_LIMIT = 12 * 1024 * 1024
HOLD_LIMIT = 32 * 1024 * 1024
STREAM_LIMIT = 40 * 1024 * 1024


def spots():
    return [(x, y, z, c) for x in range(4) for y in range(4) for z in range(4) for c in range(2)]


def coords(x, y, z, c):
    return 8 * y + 2 * z + x % 2, x // 2 * 2 + c


def device(x, y, z, c):
    blk, rep = coords(x % 4, y % 4, z % 4, c)
    return 4 * blk + rep


def levels(x, y, z, c):
    kind = sum(coords(x, y, z, c)) % 4
    level = z if kind // 2 == z % 2 else z + 1
    return kind % 2, (level + 2 * c) % 4, (level + 2 - 2 * c) % 4


def slot_table():
    table = np.zeros((128, 8), np.int32)
    for spot in spots():
        low, near, far = levels(*spot)
        base = sum(coords(*spot))
        for item in range(8):
            row = (spot[1] + item) % 4
            wanted = 8 * row + 2 * (near if item < 4 else far) + low
            table[device(*spot), item] = (wanted - base) % 32 // 4
    return table


def fetch_pairs():
    listed = []
    for x, y, z, c in spots():
        near = levels(x, y, z, c)[1]
        listed.append((device(x - c, y, near, c), device(x, y, z, c)))
    return listed


def fetched_rep(x, y, z, c):
    return coords((x - c) % 4, y, z, c)[1]


def quarter_pairs(shift):
    listed = []
    for x, y, z, c in spots():
        near = levels(x, y, z, c)[1]
        blk = device(x - c, y, near, c) // 4
        listed.append((device(x, y, z, c), 4 * blk + (fetched_rep(x, y, z, c) + shift) % 4))
    return listed


def rep_table():
    table = np.zeros((128, 1), np.int32)
    for spot in spots():
        table[device(*spot), 0] = fetched_rep(*spot)
    return table


def partner_pairs():
    return [(device(x, y, z, c), device(x + 2 * c - 1, y, z, 1 - c)) for x, y, z, c in spots()]


def ring_pairs(step):
    return [(device(x, y, z, c), device(x, y + step, z, c)) for x, y, z, c in spots()]


def params(limit=VMEM_LIMIT):
    return pltpu.CompilerParams(vmem_limit_bytes=limit)


def whole():
    return pl.BlockSpec(memory_space=pltpu.VMEM)


def order_kernel(order_ref, feat_ref, out_ref):
    rows = feat_ref.shape[0]
    step = 512
    feats = feat_ref[...]
    for start in range(0, rows, step):
        parts = []
        for inner in range(start, start + step, TILE):
            line = order_ref[0:1, inner : inner + TILE]
            parts.append(jnp.broadcast_to(line, (TILE, TILE)).T)
        column = jnp.concatenate(parts, axis=0)
        pieces = []
        for col in range(0, rows, TILE):
            level = lax.broadcasted_iota(jnp.int32, (step, TILE), 1) + col
            pieces.append((column == level).astype(jnp.float32).astype(jnp.bfloat16))
        pick = jnp.concatenate(pieces, axis=1)
        out_ref[start : start + step, :] = jnp.dot(
            pick, feats, preferred_element_type=jnp.float32
        ).astype(jnp.bfloat16)


def order_rows(order, features):
    return pl.pallas_call(
        order_kernel,
        out_shape=jax.ShapeDtypeStruct(features.shape, jnp.bfloat16),
        in_specs=[whole(), whole()],
        out_specs=whole(),
        compiler_params=params(),
    )(order, features)


def tile_copies(slots, tiles_ref, out_ref, sems):
    per_slot = out_ref.shape[0] // len(slots)
    part = per_slot // PARTS
    copies = []
    for number, slot in enumerate(slots):
        for piece in range(PARTS):
            target = number * per_slot + piece * part
            copies.append(
                pltpu.make_async_copy(
                    tiles_ref.at[pl.ds(slot * per_slot + piece * part, part)],
                    out_ref.at[pl.ds(target, part)],
                    sems.at[number * PARTS + piece],
                )
            )
    return copies


def hold_kernel(items, place_ref, tiles_ref, out_ref, sems):
    slots = [place_ref[1 + item] for item in items]
    copies = tile_copies(slots, tiles_ref, out_ref, sems)
    for copy in copies:
        copy.start()
    for copy in copies:
        copy.wait()


def hold(items, place, tiles, per_slot):
    size = len(items) * per_slot
    return pl.pallas_call(
        functools.partial(hold_kernel, items),
        out_shape=jax.ShapeDtypeStruct((size, TILE, TILE), tiles.dtype),
        grid_spec=pltpu.PrefetchScalarGridSpec(
            num_scalar_prefetch=1,
            grid=(),
            in_specs=[pl.BlockSpec(memory_space=pltpu.HBM)],
            out_specs=whole(),
            scratch_shapes=[pltpu.SemaphoreType.DMA((len(items) * PARTS,))],
        ),
        compiler_params=params(HOLD_LIMIT),
        cost_estimate=pl.CostEstimate(
            flops=0, bytes_accessed=4 * size * TILE * TILE, transcendentals=0
        ),
    )(place, tiles)


def tile_lists(key, source, target_count, zero, width, turn):
    lists, size = key.shape
    capacity = (size + target_count * (width - 1)) // width
    capacity = -(-capacity // turn) * turn
    ids = jnp.arange(size, dtype=jnp.int32)
    levels = jnp.arange(target_count, dtype=jnp.int32)
    earlier = (key[:, None, :] == key[:, :, None]) & (ids[None, :] < ids[:, None])
    rank = jnp.sum(earlier.astype(jnp.int32), axis=2)
    held = jnp.sum((key[:, None, :] == levels[:, None]).astype(jnp.int32), axis=2)
    needed = (held + width - 1) // width
    upto = levels[None, :] <= levels[:, None]
    ends = jnp.sum(jnp.where(upto, needed[:, None, :], 0), axis=2)
    base = jnp.sum(jnp.where(levels < key[:, :, None], needed[:, None, :], 0), axis=2)
    place = jnp.where(key < target_count, base * width + rank, -1)
    cells = jnp.arange(capacity * width, dtype=jnp.int32)
    hit = (place[:, None, :] == cells[:, None]).astype(jnp.int32)
    tile = jnp.sum(hit * ids, axis=2)
    origin = zero + jnp.sum(hit * (source - zero)[:, None, :], axis=2)
    groups = jnp.arange(capacity, dtype=jnp.int32)
    target = jnp.sum((ends[:, None, :] <= groups[:, None]).astype(jnp.int32), axis=2)
    code = tile * CODE + origin
    packed = jnp.concatenate([code.reshape(-1), target.reshape(-1), jnp.max(ends, axis=1)])
    return packed, capacity


def group_turns(groups, length, target_of, store, product):
    def turn(index, total):
        for lane in range(length):
            group = index * length + lane
            target = target_of(group)
            new = (group == 0) | (target != target_of(jnp.maximum(group - 1, 0)))
            fresh = product(group)
            total = jnp.where(new, fresh, total + fresh)
            store(pl.ds(pl.multiple_of(target * TILE, TILE), TILE), total)
        return total

    turns = (groups + length - 1) // length
    lax.fori_loop(0, turns, turn, jnp.zeros((TILE, TILE), jnp.float32))


def forward_kernel(pieces, lists, wave, capacity, list_ref, hold_ref, *refs):
    first = wave == 0
    x_refs, refs = refs[:pieces], refs[pieces:]
    codes = lists * capacity * FORWARD_WIDTH
    ends = codes + lists * capacity
    copies = []
    if first:
        tiles_ref = hold_ref
        total_ref, x_ref, hold_ref, sems = refs
        slots = [list_ref[ends + lists + 1 + item] for item in FORWARD_WAVES[0]]
        copies = tile_copies(slots, tiles_ref, hold_ref, sems)
        for copy in copies:
            copy.start()
        total_ref[...] = jnp.zeros_like(total_ref)
    else:
        before_ref, out_refs, (total_ref, x_ref) = refs[0], refs[1:-2], refs[-2:]
        total_ref[...] = before_ref[...].astype(jnp.bfloat16)
    start = 0
    for piece_ref in x_refs:
        x_ref[start : start + piece_ref.shape[0], :] = piece_ref[...]
        start += piece_ref.shape[0]
    x_ref[start:, :] = jnp.zeros((TILE, TILE), jnp.bfloat16)
    for copy in copies:
        copy.wait()

    def product(group):
        begin = (wave * capacity + group) * FORWARD_WIDTH
        codes = [list_ref[begin + item] for item in range(FORWARD_WIDTH)]
        left = jnp.concatenate([hold_ref[code // CODE] for code in codes], axis=1)
        starts = [pl.multiple_of(code % CODE * TILE, TILE) for code in codes]
        right = jnp.concatenate([x_ref[pl.ds(start, TILE), :] for start in starts], axis=0)
        return jnp.dot(left, right, preferred_element_type=jnp.float32)

    def store(span, total):
        if first:
            total_ref[span, :] = total
        else:
            total_ref[span, :] = (total + before_ref[span, :]).astype(jnp.bfloat16)

    group_turns(
        list_ref[ends + wave],
        FORWARD_TURN,
        lambda group: list_ref[codes + wave * capacity + group],
        store,
        product,
    )
    if not first:
        reps = len(out_refs)
        own = out_refs[0].shape[0]
        here = list_ref[ends + lists]
        for shift, out_ref in enumerate(out_refs):
            start = pl.multiple_of((here + shift) % reps * own, own)
            out_ref[...] = total_ref[pl.ds(start, own), :]


def estimate(tiles):
    return pl.CostEstimate(
        flops=8 * tiles * TILE**3, bytes_accessed=tiles * TILE * TILE * 2, transcendentals=0
    )


def forward_product(rows, lists, wave, packed, capacity, tiles, xs, before, reps):
    first = wave == 0
    total_shape = (rows + TILE, TILE)
    x_rows = sum(x.shape[0] for x in xs)
    x_scratch = pltpu.VMEM((x_rows + TILE, TILE), jnp.bfloat16)
    in_specs = [whole()] * (1 + len(xs))
    if first:
        operands = [tiles, *xs]
        in_specs[0] = pl.BlockSpec(memory_space=pltpu.HBM)
        out_shape = jax.ShapeDtypeStruct(total_shape, jnp.float32)
        out_specs = whole()
        count = len(FORWARD_WAVES[0])
        held = (tiles.shape[0] // (lists * count) * count, TILE, TILE)
        scratch = [
            x_scratch,
            pltpu.VMEM(held, jnp.bfloat16),
            pltpu.SemaphoreType.DMA((count * PARTS,)),
        ]
    else:
        operands = [tiles, *xs, before]
        in_specs.append(whole())
        out_shape = [jax.ShapeDtypeStruct((rows // reps, TILE), jnp.bfloat16)] * reps
        out_specs = [whole()] * reps
        scratch = [pltpu.VMEM(total_shape, jnp.bfloat16), x_scratch]
    return pl.pallas_call(
        functools.partial(forward_kernel, len(xs), lists, wave, capacity),
        out_shape=out_shape,
        grid_spec=pltpu.PrefetchScalarGridSpec(
            num_scalar_prefetch=1,
            grid=(),
            in_specs=in_specs,
            out_specs=out_specs,
            scratch_shapes=scratch,
        ),
        compiler_params=params(STREAM_LIMIT if first else VMEM_LIMIT),
        cost_estimate=estimate(x_rows // rows * 80),
    )(packed, *operands)


def dense_kernel(*refs):
    part_refs, (weight_ref, upstream_ref, act_ref, pay_ref) = refs[:-4], refs[-4:]
    rows = upstream_ref.shape[0]
    total = part_refs[0][...].astype(jnp.float32)
    for part_ref in part_refs[1:]:
        total = total + part_ref[...].astype(jnp.float32)
    aggregated = total.astype(jnp.bfloat16)
    weight = weight_ref[...]
    pre = jnp.dot(aggregated, weight, preferred_element_type=jnp.float32)
    gate = jax.nn.sigmoid(pre)
    act_ref[...] = (pre * gate).astype(jnp.bfloat16)
    grad_pre = (
        upstream_ref[...].astype(jnp.float32) * gate * (1.0 + pre * (1.0 - gate))
    ).astype(jnp.bfloat16)
    back = lax.dot_general(
        weight, grad_pre, (((1,), (1,)), ((), ())), preferred_element_type=jnp.float32
    ).astype(jnp.bfloat16)
    for block in range(rows // TILE):
        pay_ref[block * TILE : (block + 1) * TILE, :] = back[:, block * TILE : (block + 1) * TILE]
    local = lax.dot_general(
        aggregated, grad_pre, (((0,), (0,)), ((), ())), preferred_element_type=jnp.float32
    ).astype(jnp.bfloat16)
    for half in range(weight.shape[1] // TILE):
        pay_ref[rows + half * TILE : rows + (half + 1) * TILE, :] = local[
            :, half * TILE : (half + 1) * TILE
        ]


def dense_layer(parts, weight, upstream):
    rows, hidden = upstream.shape
    pay_rows = rows + hidden // TILE * weight.shape[0]
    return pl.pallas_call(
        dense_kernel,
        out_shape=(
            jax.ShapeDtypeStruct((rows, hidden), jnp.bfloat16),
            jax.ShapeDtypeStruct((pay_rows, TILE), jnp.bfloat16),
        ),
        in_specs=[whole()] * (len(parts) + 2),
        out_specs=(whole(), whole()),
        compiler_params=params(),
    )(*parts, weight, upstream)


def backward_kernel(sizes, rows, lists, first, capacity, list_ref, hold_ref, *refs):
    pay_refs, out_refs = refs[: -2 - len(sizes)], refs[-2 - len(sizes) : -2]
    count = sum(sizes)
    spots_of = [(number, item) for number, size in enumerate(sizes) for item in range(size)]
    total_ref, back_ref = refs[-2:]
    reps = len(pay_refs)
    own = rows // reps
    per_slot = hold_ref.shape[0] // count
    codes = lists * capacity * BACKWARD_WIDTH
    ends = codes + lists * capacity
    place = ends + lists
    here = list_ref[place]
    for shift, pay_ref in enumerate(pay_refs):
        start = pl.multiple_of((here + reps - shift) % reps * own, own)
        back_ref[pl.ds(start, own), :] = pay_ref[:own, :]
    back_ref[rows:, :] = jnp.zeros((TILE, TILE), jnp.bfloat16)
    total_ref[...] = jnp.zeros_like(total_ref)
    if out_refs[0].shape[0] > sizes[0] * rows:
        ride = pay_refs[0][own:, :].astype(jnp.float32)
        for pay_ref in pay_refs[1:]:
            ride = ride + pay_ref[own:, :].astype(jnp.float32)
        out_refs[0][sizes[0] * rows :, :] = ride.astype(jnp.bfloat16)
    for number in range(0, count, PAIR):
        listed = first + number // PAIR

        def product(group, listed=listed, number=number):
            begin = (listed * capacity + group) * BACKWARD_WIDTH
            items = [list_ref[begin + item] for item in range(BACKWARD_WIDTH)]
            starts = [pl.multiple_of(code % CODE * TILE, TILE) for code in items]
            left = jnp.concatenate([back_ref[pl.ds(start, TILE), :] for start in starts], axis=1)
            right = jnp.concatenate(
                [hold_ref[number * per_slot + code // CODE] for code in items], axis=0
            )
            return jnp.dot(left, right, preferred_element_type=jnp.float32)

        def target_of(group, listed=listed):
            return list_ref[codes + listed * capacity + group]

        def store(span, total):
            total_ref[span, :] = total.astype(jnp.bfloat16)

        group_turns(list_ref[ends + listed], BACKWARD_TURN, target_of, store, product)
        for item in range(PAIR):
            target, spot = spots_of[number + item]
            out_refs[target][spot * rows : (spot + 1) * rows, :] = total_ref[
                item * rows : (item + 1) * rows, :
            ]
        if number + PAIR < count:
            total_ref[...] = jnp.zeros_like(total_ref)


def backward_product(sizes, rows, lists, first, packed, capacity, held, pays):
    out_rows = [size * rows for size in sizes]
    if first == 0:
        out_rows[0] += pays[0].shape[0] - rows // len(pays)
    return pl.pallas_call(
        functools.partial(backward_kernel, sizes, rows, lists, first, capacity),
        out_shape=[jax.ShapeDtypeStruct((size, TILE), jnp.bfloat16) for size in out_rows],
        grid_spec=pltpu.PrefetchScalarGridSpec(
            num_scalar_prefetch=1,
            grid=(),
            in_specs=[whole()] * (1 + len(pays)),
            out_specs=[whole()] * len(sizes),
            scratch_shapes=[
                pltpu.VMEM((PAIR * rows + TILE, TILE), jnp.bfloat16),
                pltpu.VMEM((rows + TILE, TILE), jnp.bfloat16),
            ],
        ),
        compiler_params=params(),
        cost_estimate=estimate(held.shape[0]),
    )(packed, held, *pays)


def restore_kernel(place_ref, order_ref, home_ref, *refs):
    out_refs, part_ref = refs[:-1], refs[-1]
    rows = order_ref.shape[1]
    reps = len(out_refs)
    own = rows // reps
    for block in range(rows // TILE):
        span = slice(block * TILE, (block + 1) * TILE)
        part_ref[span, :] = home_ref[span, :].astype(jnp.float32).T.astype(jnp.bfloat16)
    order = order_ref[...]
    part = part_ref[...]
    for shift, out_ref in enumerate(out_refs):
        start = (place_ref[0] + shift) % reps * own
        level = lax.broadcasted_iota(jnp.int32, (own, rows), 0) + start
        pick = (jnp.broadcast_to(order, (own, rows)) == level).astype(jnp.float32)
        out_ref[:own, :] = jnp.dot(
            pick.astype(jnp.bfloat16), part, preferred_element_type=jnp.float32
        ).astype(jnp.bfloat16)
        out_ref[own:, :] = home_ref[rows:, :]


def restore(place, order, home, reps):
    rows = order.shape[1]
    out_rows = rows // reps + home.shape[0] - rows
    out_shape = jax.ShapeDtypeStruct((out_rows, TILE), jnp.bfloat16)
    return pl.pallas_call(
        restore_kernel,
        out_shape=[out_shape] * reps,
        grid_spec=pltpu.PrefetchScalarGridSpec(
            num_scalar_prefetch=1,
            grid=(),
            in_specs=[whole()] * 2,
            out_specs=[whole()] * reps,
            scratch_shapes=[pltpu.VMEM((rows, TILE), jnp.bfloat16)],
        ),
        compiler_params=params(),
    )(place, order, home)


def added(*values):
    return sum(value.astype(jnp.float32) for value in values).astype(jnp.bfloat16)


def per_device(features, node_order, adj_values, adj_rows, adj_cols, tile_count, weight, upstream):
    reps = lax.axis_size("rep")
    slices = lax.axis_size("blk")
    steps = slices // reps
    rows_dev = features.shape[0]
    blocks = rows_dev // TILE
    both = ("blk", "rep")
    row_ids, col_ids, counts = adj_rows[0, 0], adj_cols[0, 0], tile_count[0, 0]
    per_slot = row_ids.shape[1]
    tiles = adj_values.reshape((-1, TILE, TILE))
    own_rep = lax.axis_index("rep").astype(jnp.int32).reshape(1)

    here = lax.axis_index("blk") * reps + lax.axis_index("rep")
    slots = lax.dynamic_index_in_dim(jnp.asarray(slot_table()), here, 0, keepdims=False)
    place = jnp.concatenate([own_rep, slots])
    home_rep = lax.dynamic_index_in_dim(jnp.asarray(rep_table()), here, 0, keepdims=False)
    half = rows_dev // 2

    def moved(value, listed):
        return lax.ppermute(value, both, listed)

    def up(value):
        return moved(value, ring_pairs(1))

    def down(value):
        return moved(value, ring_pairs(-1))

    def swapped(value):
        return moved(value, partner_pairs())

    def to_reps(values):
        received = [values[0]]
        for shift in range(1, reps):
            along = [(rep, (rep + shift) % reps) for rep in range(reps)]
            received.append(lax.ppermute(values[shift], "rep", along))
        return received

    blocked = order_rows(node_order, features)
    near = moved(blocked, fetch_pairs())
    alive = jnp.arange(per_slot, dtype=jnp.int32)[None, :] < counts[:, None]
    cells = jnp.take(jnp.where(alive, row_ids * CODE + col_ids, -1), slots, axis=0)

    def split(cells, items):
        chosen = jnp.concatenate([cells[item : item + 1] for item in items])
        return chosen >= 0, chosen // CODE, chosen % CODE

    waves = len(FORWARD_WAVES)
    alive, rows_of, cols_of = split(cells, sum(FORWARD_WAVES, ()))
    offsets = jnp.arange(steps, dtype=jnp.int32)[:, None] % (steps // waves) * blocks
    forward_list, forward_capacity = tile_lists(
        jnp.where(alive, rows_of, blocks).reshape(waves, -1),
        (cols_of + offsets).reshape(waves, -1),
        blocks,
        steps // waves * blocks,
        FORWARD_WIDTH,
        FORWARD_TURN,
    )
    forward_list = jnp.concatenate([forward_list, place])
    late_cells, near = lax.optimization_barrier((cells, near))
    lists = steps // PAIR
    alive, rows_of, cols_of = split(late_cells, sum(BACKWARD_WAVES, ()))
    offsets = jnp.arange(steps, dtype=jnp.int32)[:, None] % PAIR * blocks
    packed, capacity = tile_lists(
        jnp.where(alive, cols_of + offsets, PAIR * blocks).reshape(lists, -1),
        rows_of.reshape(lists, -1),
        PAIR * blocks,
        blocks,
        BACKWARD_WIDTH,
        BACKWARD_TURN,
    )
    packed = jnp.concatenate([packed, own_rep])
    above, below = down(near), up(near)
    ready, packed = lax.optimization_barrier((near, packed))
    far = swapped(ready)
    above, below, far, forward_list, packed = lax.optimization_barrier(
        (above, below, far, forward_list, packed)
    )
    middle = [down(above[:half]), up(below[half:])]
    known, far = lax.optimization_barrier((place, far))
    held = hold(FORWARD_WAVES[1], known, tiles, per_slot)
    xs = [near, above, below, *middle]
    total = forward_product(
        rows_dev, waves, 0, forward_list, forward_capacity, tiles, xs, None, reps
    )
    xs = [far, swapped(above), swapped(below), *[swapped(value) for value in middle]]
    total = list(
        forward_product(
            rows_dev, waves, 1, forward_list, forward_capacity, held, xs, total, reps
        )
    )
    known, total[0] = lax.optimization_barrier((place, total[0]))
    shared = to_reps(total)
    holds = [hold(BACKWARD_WAVES[0], known, tiles, per_slot)]
    shared[1], holds[0] = lax.optimization_barrier((shared[1], holds[0]))
    activations, pay = dense_layer(shared, weight, upstream)
    known, pay = lax.optimization_barrier((place, pay))
    pays = to_reps([pay] * reps)
    holds.append(hold(BACKWARD_WAVES[1], known, tiles, per_slot))
    packed, holds = lax.optimization_barrier((packed, holds))

    def products(wave, packed):
        sizes = BACKWARD_OUTPUTS[wave]
        first = wave * sum(sizes) // PAIR
        return list(
            backward_product(sizes, rows_dev, lists, first, packed, capacity, holds[wave], pays)
        )

    others = products(0, packed)
    packed, others[2] = lax.optimization_barrier((packed, others[2]))
    returned = swapped(others[0])
    sides = swapped(others[1])
    last = swapped(others[2])
    mine = products(1, packed)
    two = added(mine[2], returned[:rows_dev])
    ride = added(others[0][rows_dev:], returned[rows_dev:])
    from_below, from_above, later_order = lax.optimization_barrier(
        (
            up(jnp.concatenate([two[:half], ride])),
            down(jnp.concatenate([two[half:], ride])),
            node_order,
        )
    )
    near_order = moved(later_order, fetch_pairs())
    one = jnp.concatenate(
        [
            added(mine[1][:half], sides[:half], from_below[:half]),
            added(mine[1][half:], sides[half:rows_dev]),
            from_below[half:],
        ]
    )
    three = jnp.concatenate(
        [
            added(mine[3][:half], sides[rows_dev : rows_dev + half]),
            added(mine[3][half:], sides[rows_dev + half :], from_above[:half]),
        ]
    )
    below_sum, above_sum = up(one), down(three)
    ended = jnp.concatenate(
        [
            added(mine[0], last, below_sum[:rows_dev], above_sum),
            added(ride, from_below[half:], from_above[half:], below_sum[rows_dev:]),
        ]
    )
    quarters = restore(home_rep, near_order, ended, reps)
    terms = [moved(value, quarter_pairs(shift)) for shift, value in enumerate(quarters)]
    own = rows_dev // reps
    grad_features = added(*[term[:own] for term in terms])
    grad_weight = sum(term[own:].astype(jnp.float32) for term in terms)
    stacked = grad_weight.reshape(weight.shape[1] // TILE, weight.shape[0], TILE)
    grad_weight = jnp.concatenate([stacked[half] for half in range(stacked.shape[0])], axis=1)
    return (activations, grad_weight, grad_features)


def solution(mesh):
    placed = (
        P("blk", None),
        P("blk", None),
        P("blk", "rep", None, None, None, None),
        P("blk", "rep", None, None),
        P("blk", "rep", None, None),
        P("blk", "rep", None),
        P(),
        P(("blk", "rep"), None),
    )
    return jax.shard_map(
        per_device,
        mesh=mesh,
        in_specs=placed,
        out_specs=(P(("blk", "rep"), None), P(), P(("blk", "rep"), None)),
        check_vma=False,
    )
```

```python
import functools

import jax
import jax.numpy as jnp
import numpy as np
from jax import lax
from jax.experimental import pallas as pl
from jax.experimental.pallas import tpu as pltpu
from jax.sharding import PartitionSpec as P

TILE = 128
FORWARD_TURN = 8
BACKWARD_TURN = 16
FORWARD_WIDTH = 4
BACKWARD_WIDTH = 2
FORWARD_WAVES = ((0, 1, 3, 2), (4, 5, 7, 6))
BACKWARD_WAVES = ((6, 5, 7, 4), (0, 1, 2, 3))
BACKWARD_OUTPUTS = ((1, 2, 1), (1, 1, 1, 1))
PAIR = 2
PARTS = 4
CODE = 256
VMEM_LIMIT = 12 * 1024 * 1024
HOLD_LIMIT = 32 * 1024 * 1024
STREAM_LIMIT = 40 * 1024 * 1024


def spots():
    return [(x, y, z, c) for x in range(4) for y in range(4) for z in range(4) for c in range(2)]


def coords(x, y, z, c):
    return 8 * y + 2 * z + x % 2, x // 2 * 2 + c


def device(x, y, z, c):
    blk, rep = coords(x % 4, y % 4, z % 4, c)
    return 4 * blk + rep


def levels(x, y, z, c):
    kind = sum(coords(x, y, z, c)) % 4
    level = z if kind // 2 == z % 2 else z + 1
    return kind % 2, (level + 2 * c) % 4, (level + 2 - 2 * c) % 4


def slot_table():
    table = np.zeros((128, 8), np.int32)
    for spot in spots():
        low, near, far = levels(*spot)
        base = sum(coords(*spot))
        for item in range(8):
            row = (spot[1] + item) % 4
            wanted = 8 * row + 2 * (near if item < 4 else far) + low
            table[device(*spot), item] = (wanted - base) % 32 // 4
    return table


def fetch_pairs():
    listed = []
    for x, y, z, c in spots():
        near = levels(x, y, z, c)[1]
        listed.append((device(x - c, y, near, c), device(x, y, z, c)))
    return listed


def fetched_rep(x, y, z, c):
    return coords((x - c) % 4, y, z, c)[1]


def quarter_pairs(shift):
    listed = []
    for x, y, z, c in spots():
        near = levels(x, y, z, c)[1]
        blk = device(x - c, y, near, c) // 4
        listed.append((device(x, y, z, c), 4 * blk + (fetched_rep(x, y, z, c) + shift) % 4))
    return listed


def rep_table():
    table = np.zeros((128, 1), np.int32)
    for spot in spots():
        table[device(*spot), 0] = fetched_rep(*spot)
    return table


def partner_pairs():
    return [(device(x, y, z, c), device(x + 2 * c - 1, y, z, 1 - c)) for x, y, z, c in spots()]


def ring_pairs(step):
    return [(device(x, y, z, c), device(x, y + step, z, c)) for x, y, z, c in spots()]


def params(limit=VMEM_LIMIT):
    return pltpu.CompilerParams(vmem_limit_bytes=limit)


def whole():
    return pl.BlockSpec(memory_space=pltpu.VMEM)


def order_kernel(order_ref, feat_ref, out_ref):
    rows = feat_ref.shape[0]
    step = 512
    feats = feat_ref[...]
    for start in range(0, rows, step):
        parts = []
        for inner in range(start, start + step, TILE):
            line = order_ref[0:1, inner : inner + TILE]
            parts.append(jnp.broadcast_to(line, (TILE, TILE)).T)
        column = jnp.concatenate(parts, axis=0)
        pieces = []
        for col in range(0, rows, TILE):
            level = lax.broadcasted_iota(jnp.int32, (step, TILE), 1) + col
            pieces.append((column == level).astype(jnp.float32).astype(jnp.bfloat16))
        pick = jnp.concatenate(pieces, axis=1)
        out_ref[start : start + step, :] = jnp.dot(
            pick, feats, preferred_element_type=jnp.float32
        ).astype(jnp.bfloat16)


def order_rows(order, features):
    return pl.pallas_call(
        order_kernel,
        out_shape=jax.ShapeDtypeStruct(features.shape, jnp.bfloat16),
        in_specs=[whole(), whole()],
        out_specs=whole(),
        compiler_params=params(),
    )(order, features)


def tile_copies(slots, tiles_ref, out_ref, sems):
    per_slot = out_ref.shape[0] // len(slots)
    part = per_slot // PARTS
    copies = []
    for number, slot in enumerate(slots):
        for piece in range(PARTS):
            target = number * per_slot + piece * part
            copies.append(
                pltpu.make_async_copy(
                    tiles_ref.at[pl.ds(slot * per_slot + piece * part, part)],
                    out_ref.at[pl.ds(target, part)],
                    sems.at[number * PARTS + piece],
                )
            )
    return copies


def hold_kernel(items, place_ref, tiles_ref, out_ref, sems):
    slots = [place_ref[1 + item] for item in items]
    copies = tile_copies(slots, tiles_ref, out_ref, sems)
    for copy in copies:
        copy.start()
    for copy in copies:
        copy.wait()


def hold(items, place, tiles, per_slot):
    size = len(items) * per_slot
    return pl.pallas_call(
        functools.partial(hold_kernel, items),
        out_shape=jax.ShapeDtypeStruct((size, TILE, TILE), tiles.dtype),
        grid_spec=pltpu.PrefetchScalarGridSpec(
            num_scalar_prefetch=1,
            grid=(),
            in_specs=[pl.BlockSpec(memory_space=pltpu.HBM)],
            out_specs=whole(),
            scratch_shapes=[pltpu.SemaphoreType.DMA((len(items) * PARTS,))],
        ),
        compiler_params=params(HOLD_LIMIT),
        cost_estimate=pl.CostEstimate(
            flops=0, bytes_accessed=4 * size * TILE * TILE, transcendentals=0
        ),
    )(place, tiles)


def tile_lists(key, source, target_count, zero, width, turn):
    lists, size = key.shape
    capacity = (size + target_count * (width - 1)) // width
    capacity = -(-capacity // turn) * turn
    ids = jnp.arange(size, dtype=jnp.int32)
    levels = jnp.arange(target_count, dtype=jnp.int32)
    earlier = (key[:, None, :] == key[:, :, None]) & (ids[None, :] < ids[:, None])
    rank = jnp.sum(earlier.astype(jnp.int32), axis=2)
    held = jnp.sum((key[:, None, :] == levels[:, None]).astype(jnp.int32), axis=2)
    needed = (held + width - 1) // width
    upto = levels[None, :] <= levels[:, None]
    ends = jnp.sum(jnp.where(upto, needed[:, None, :], 0), axis=2)
    base = jnp.sum(jnp.where(levels < key[:, :, None], needed[:, None, :], 0), axis=2)
    place = jnp.where(key < target_count, base * width + rank, -1)
    cells = jnp.arange(capacity * width, dtype=jnp.int32)
    hit = (place[:, None, :] == cells[:, None]).astype(jnp.int32)
    tile = jnp.sum(hit * ids, axis=2)
    origin = zero + jnp.sum(hit * (source - zero)[:, None, :], axis=2)
    groups = jnp.arange(capacity, dtype=jnp.int32)
    target = jnp.sum((ends[:, None, :] <= groups[:, None]).astype(jnp.int32), axis=2)
    code = tile * CODE + origin
    packed = jnp.concatenate([code.reshape(-1), target.reshape(-1), jnp.max(ends, axis=1)])
    return packed, capacity


def group_turns(groups, length, target_of, store, product):
    def turn(index, total):
        for lane in range(length):
            group = index * length + lane
            target = target_of(group)
            new = (group == 0) | (target != target_of(jnp.maximum(group - 1, 0)))
            fresh = product(group)
            total = jnp.where(new, fresh, total + fresh)
            store(pl.ds(pl.multiple_of(target * TILE, TILE), TILE), total)
        return total

    turns = (groups + length - 1) // length
    lax.fori_loop(0, turns, turn, jnp.zeros((TILE, TILE), jnp.float32))


def forward_kernel(pieces, lists, wave, capacity, list_ref, hold_ref, *refs):
    first = wave == 0
    x_refs, refs = refs[:pieces], refs[pieces:]
    codes = lists * capacity * FORWARD_WIDTH
    ends = codes + lists * capacity
    copies = []
    if first:
        tiles_ref = hold_ref
        total_ref, x_ref, hold_ref, sems = refs
        slots = [list_ref[ends + lists + 1 + item] for item in FORWARD_WAVES[0]]
        copies = tile_copies(slots, tiles_ref, hold_ref, sems)
        for copy in copies:
            copy.start()
        total_ref[...] = jnp.zeros_like(total_ref)
    else:
        before_ref, out_refs, (total_ref, x_ref) = refs[0], refs[1:-2], refs[-2:]
        total_ref[...] = before_ref[...].astype(jnp.bfloat16)
    start = 0
    for piece_ref in x_refs:
        x_ref[start : start + piece_ref.shape[0], :] = piece_ref[...]
        start += piece_ref.shape[0]
    x_ref[start:, :] = jnp.zeros((TILE, TILE), jnp.bfloat16)
    for copy in copies:
        copy.wait()

    def product(group):
        begin = (wave * capacity + group) * FORWARD_WIDTH
        codes = [list_ref[begin + item] for item in range(FORWARD_WIDTH)]
        left = jnp.concatenate([hold_ref[code // CODE] for code in codes], axis=1)
        starts = [pl.multiple_of(code % CODE * TILE, TILE) for code in codes]
        right = jnp.concatenate([x_ref[pl.ds(start, TILE), :] for start in starts], axis=0)
        return jnp.dot(left, right, preferred_element_type=jnp.float32)

    def store(span, total):
        if first:
            total_ref[span, :] = total
        else:
            total_ref[span, :] = (total + before_ref[span, :]).astype(jnp.bfloat16)

    group_turns(
        list_ref[ends + wave],
        FORWARD_TURN,
        lambda group: list_ref[codes + wave * capacity + group],
        store,
        product,
    )
    if not first:
        reps = len(out_refs)
        own = out_refs[0].shape[0]
        here = list_ref[ends + lists]
        for shift, out_ref in enumerate(out_refs):
            start = pl.multiple_of((here ^ shift) * own, own)
            out_ref[...] = total_ref[pl.ds(start, own), :]


def estimate(tiles):
    return pl.CostEstimate(
        flops=8 * tiles * TILE**3, bytes_accessed=tiles * TILE * TILE * 2, transcendentals=0
    )


def forward_product(rows, lists, wave, packed, capacity, tiles, xs, before, reps):
    first = wave == 0
    total_shape = (rows + TILE, TILE)
    x_rows = sum(x.shape[0] for x in xs)
    x_scratch = pltpu.VMEM((x_rows + TILE, TILE), jnp.bfloat16)
    in_specs = [whole()] * (1 + len(xs))
    if first:
        operands = [tiles, *xs]
        in_specs[0] = pl.BlockSpec(memory_space=pltpu.HBM)
        out_shape = jax.ShapeDtypeStruct(total_shape, jnp.float32)
        out_specs = whole()
        count = len(FORWARD_WAVES[0])
        held = (tiles.shape[0] // (lists * count) * count, TILE, TILE)
        scratch = [
            x_scratch,
            pltpu.VMEM(held, jnp.bfloat16),
            pltpu.SemaphoreType.DMA((count * PARTS,)),
        ]
    else:
        operands = [tiles, *xs, before]
        in_specs.append(whole())
        out_shape = [jax.ShapeDtypeStruct((rows // reps, TILE), jnp.bfloat16)] * reps
        out_specs = [whole()] * reps
        scratch = [pltpu.VMEM(total_shape, jnp.bfloat16), x_scratch]
    return pl.pallas_call(
        functools.partial(forward_kernel, len(xs), lists, wave, capacity),
        out_shape=out_shape,
        grid_spec=pltpu.PrefetchScalarGridSpec(
            num_scalar_prefetch=1,
            grid=(),
            in_specs=in_specs,
            out_specs=out_specs,
            scratch_shapes=scratch,
        ),
        compiler_params=params(STREAM_LIMIT if first else VMEM_LIMIT),
        cost_estimate=estimate(x_rows // rows * 80),
    )(packed, *operands)


def dense_kernel(*refs):
    part_refs, (weight_ref, upstream_ref, act_ref, pay_ref) = refs[:-4], refs[-4:]
    rows = upstream_ref.shape[0]
    total = part_refs[0][...].astype(jnp.float32)
    for part_ref in part_refs[1:]:
        total = total + part_ref[...].astype(jnp.float32)
    aggregated = total.astype(jnp.bfloat16)
    weight = weight_ref[...]
    pre = jnp.dot(aggregated, weight, preferred_element_type=jnp.float32)
    gate = jax.nn.sigmoid(pre)
    act_ref[...] = (pre * gate).astype(jnp.bfloat16)
    grad_pre = (
        upstream_ref[...].astype(jnp.float32) * gate * (1.0 + pre * (1.0 - gate))
    ).astype(jnp.bfloat16)
    back = lax.dot_general(
        weight, grad_pre, (((1,), (1,)), ((), ())), preferred_element_type=jnp.float32
    ).astype(jnp.bfloat16)
    for block in range(rows // TILE):
        pay_ref[block * TILE : (block + 1) * TILE, :] = back[:, block * TILE : (block + 1) * TILE]
    local = lax.dot_general(
        aggregated, grad_pre, (((0,), (0,)), ((), ())), preferred_element_type=jnp.float32
    ).astype(jnp.bfloat16)
    for half in range(weight.shape[1] // TILE):
        pay_ref[rows + half * TILE : rows + (half + 1) * TILE, :] = local[
            :, half * TILE : (half + 1) * TILE
        ]


def dense_layer(parts, weight, upstream):
    rows, hidden = upstream.shape
    pay_rows = rows + hidden // TILE * weight.shape[0]
    return pl.pallas_call(
        dense_kernel,
        out_shape=(
            jax.ShapeDtypeStruct((rows, hidden), jnp.bfloat16),
            jax.ShapeDtypeStruct((pay_rows, TILE), jnp.bfloat16),
        ),
        in_specs=[whole()] * (len(parts) + 2),
        out_specs=(whole(), whole()),
        compiler_params=params(),
    )(*parts, weight, upstream)


def backward_kernel(sizes, rows, lists, first, capacity, list_ref, hold_ref, *refs):
    pay_refs, out_refs = refs[: -2 - len(sizes)], refs[-2 - len(sizes) : -2]
    count = sum(sizes)
    spots_of = [(number, item) for number, size in enumerate(sizes) for item in range(size)]
    total_ref, back_ref = refs[-2:]
    reps = len(pay_refs)
    own = rows // reps
    per_slot = hold_ref.shape[0] // count
    codes = lists * capacity * BACKWARD_WIDTH
    ends = codes + lists * capacity
    place = ends + lists
    here = list_ref[place]
    for shift, pay_ref in enumerate(pay_refs):
        start = pl.multiple_of((here ^ shift) * own, own)
        back_ref[pl.ds(start, own), :] = pay_ref[:own, :]
    back_ref[rows:, :] = jnp.zeros((TILE, TILE), jnp.bfloat16)
    total_ref[...] = jnp.zeros_like(total_ref)
    if out_refs[0].shape[0] > sizes[0] * rows:
        ride = pay_refs[0][own:, :].astype(jnp.float32)
        for pay_ref in pay_refs[1:]:
            ride = ride + pay_ref[own:, :].astype(jnp.float32)
        out_refs[0][sizes[0] * rows :, :] = ride.astype(jnp.bfloat16)
    for number in range(0, count, PAIR):
        listed = first + number // PAIR

        def product(group, listed=listed, number=number):
            begin = (listed * capacity + group) * BACKWARD_WIDTH
            items = [list_ref[begin + item] for item in range(BACKWARD_WIDTH)]
            starts = [pl.multiple_of(code % CODE * TILE, TILE) for code in items]
            left = jnp.concatenate([back_ref[pl.ds(start, TILE), :] for start in starts], axis=1)
            right = jnp.concatenate(
                [hold_ref[number * per_slot + code // CODE] for code in items], axis=0
            )
            return jnp.dot(left, right, preferred_element_type=jnp.float32)

        def target_of(group, listed=listed):
            return list_ref[codes + listed * capacity + group]

        def store(span, total):
            total_ref[span, :] = total.astype(jnp.bfloat16)

        group_turns(list_ref[ends + listed], BACKWARD_TURN, target_of, store, product)
        for item in range(PAIR):
            target, spot = spots_of[number + item]
            out_refs[target][spot * rows : (spot + 1) * rows, :] = total_ref[
                item * rows : (item + 1) * rows, :
            ]
        if number + PAIR < count:
            total_ref[...] = jnp.zeros_like(total_ref)


def backward_product(sizes, rows, lists, first, packed, capacity, held, pays):
    out_rows = [size * rows for size in sizes]
    if first == 0:
        out_rows[0] += pays[0].shape[0] - rows // len(pays)
    return pl.pallas_call(
        functools.partial(backward_kernel, sizes, rows, lists, first, capacity),
        out_shape=[jax.ShapeDtypeStruct((size, TILE), jnp.bfloat16) for size in out_rows],
        grid_spec=pltpu.PrefetchScalarGridSpec(
            num_scalar_prefetch=1,
            grid=(),
            in_specs=[whole()] * (1 + len(pays)),
            out_specs=[whole()] * len(sizes),
            scratch_shapes=[
                pltpu.VMEM((PAIR * rows + TILE, TILE), jnp.bfloat16),
                pltpu.VMEM((rows + TILE, TILE), jnp.bfloat16),
            ],
        ),
        compiler_params=params(),
        cost_estimate=estimate(held.shape[0]),
    )(packed, held, *pays)


def restore_kernel(place_ref, order_ref, home_ref, *refs):
    out_refs, part_ref = refs[:-1], refs[-1]
    rows = order_ref.shape[1]
    reps = len(out_refs)
    own = rows // reps
    for block in range(rows // TILE):
        span = slice(block * TILE, (block + 1) * TILE)
        part_ref[span, :] = home_ref[span, :].astype(jnp.float32).T.astype(jnp.bfloat16)
    order = order_ref[...]
    part = part_ref[...]
    for shift, out_ref in enumerate(out_refs):
        start = (place_ref[0] + shift) % reps * own
        level = lax.broadcasted_iota(jnp.int32, (own, rows), 0) + start
        pick = (jnp.broadcast_to(order, (own, rows)) == level).astype(jnp.float32)
        out_ref[:own, :] = jnp.dot(
            pick.astype(jnp.bfloat16), part, preferred_element_type=jnp.float32
        ).astype(jnp.bfloat16)
        out_ref[own:, :] = home_ref[rows:, :]


def restore(place, order, home, reps):
    rows = order.shape[1]
    out_rows = rows // reps + home.shape[0] - rows
    out_shape = jax.ShapeDtypeStruct((out_rows, TILE), jnp.bfloat16)
    return pl.pallas_call(
        restore_kernel,
        out_shape=[out_shape] * reps,
        grid_spec=pltpu.PrefetchScalarGridSpec(
            num_scalar_prefetch=1,
            grid=(),
            in_specs=[whole()] * 2,
            out_specs=[whole()] * reps,
            scratch_shapes=[pltpu.VMEM((rows, TILE), jnp.bfloat16)],
        ),
        compiler_params=params(),
    )(place, order, home)


def added(*values):
    return sum(value.astype(jnp.float32) for value in values).astype(jnp.bfloat16)


def per_device(features, node_order, adj_values, adj_rows, adj_cols, tile_count, weight, upstream):
    reps = lax.axis_size("rep")
    slices = lax.axis_size("blk")
    steps = slices // reps
    rows_dev = features.shape[0]
    blocks = rows_dev // TILE
    both = ("blk", "rep")
    row_ids, col_ids, counts = adj_rows[0, 0], adj_cols[0, 0], tile_count[0, 0]
    per_slot = row_ids.shape[1]
    tiles = adj_values.reshape((-1, TILE, TILE))
    own_rep = lax.axis_index("rep").astype(jnp.int32).reshape(1)

    here = lax.axis_index("blk") * reps + lax.axis_index("rep")
    slots = lax.dynamic_index_in_dim(jnp.asarray(slot_table()), here, 0, keepdims=False)
    place = jnp.concatenate([own_rep, slots])
    home_rep = lax.dynamic_index_in_dim(jnp.asarray(rep_table()), here, 0, keepdims=False)
    half = rows_dev // 2

    def moved(value, listed):
        return lax.ppermute(value, both, listed)

    def up(value):
        return moved(value, ring_pairs(1))

    def down(value):
        return moved(value, ring_pairs(-1))

    def swapped(value):
        return moved(value, partner_pairs())

    def to_reps(values):
        received = [values[0]]
        for shift in range(1, reps):
            along = [(rep, rep ^ shift) for rep in range(reps)]
            received.append(lax.ppermute(values[shift], "rep", along))
        return received

    blocked = order_rows(node_order, features)
    near = moved(blocked, fetch_pairs())
    alive = jnp.arange(per_slot, dtype=jnp.int32)[None, :] < counts[:, None]
    cells = jnp.take(jnp.where(alive, row_ids * CODE + col_ids, -1), slots, axis=0)

    def split(cells, items):
        chosen = jnp.concatenate([cells[item : item + 1] for item in items])
        return chosen >= 0, chosen // CODE, chosen % CODE

    waves = len(FORWARD_WAVES)
    alive, rows_of, cols_of = split(cells, sum(FORWARD_WAVES, ()))
    offsets = jnp.arange(steps, dtype=jnp.int32)[:, None] % (steps // waves) * blocks
    forward_list, forward_capacity = tile_lists(
        jnp.where(alive, rows_of, blocks).reshape(waves, -1),
        (cols_of + offsets).reshape(waves, -1),
        blocks,
        steps // waves * blocks,
        FORWARD_WIDTH,
        FORWARD_TURN,
    )
    forward_list = jnp.concatenate([forward_list, place])
    late_cells, near = lax.optimization_barrier((cells, near))
    lists = steps // PAIR
    alive, rows_of, cols_of = split(late_cells, sum(BACKWARD_WAVES, ()))
    offsets = jnp.arange(steps, dtype=jnp.int32)[:, None] % PAIR * blocks
    packed, capacity = tile_lists(
        jnp.where(alive, cols_of + offsets, PAIR * blocks).reshape(lists, -1),
        rows_of.reshape(lists, -1),
        PAIR * blocks,
        blocks,
        BACKWARD_WIDTH,
        BACKWARD_TURN,
    )
    packed = jnp.concatenate([packed, own_rep])
    above, below = down(near), up(near)
    ready, packed = lax.optimization_barrier((near, packed))
    far = swapped(ready)
    above, below, far, forward_list, packed = lax.optimization_barrier(
        (above, below, far, forward_list, packed)
    )
    middle = [down(above[:half]), up(below[half:])]
    known, far = lax.optimization_barrier((place, far))
    held = hold(FORWARD_WAVES[1], known, tiles, per_slot)
    xs = [near, above, below, *middle]
    total = forward_product(
        rows_dev, waves, 0, forward_list, forward_capacity, tiles, xs, None, reps
    )
    xs = [far, swapped(above), swapped(below), *[swapped(value) for value in middle]]
    total = list(
        forward_product(
            rows_dev, waves, 1, forward_list, forward_capacity, held, xs, total, reps
        )
    )
    known, total[0] = lax.optimization_barrier((place, total[0]))
    shared = to_reps(total)
    holds = [hold(BACKWARD_WAVES[0], known, tiles, per_slot)]
    shared[1], holds[0] = lax.optimization_barrier((shared[1], holds[0]))
    activations, pay = dense_layer(shared, weight, upstream)
    known, pay = lax.optimization_barrier((place, pay))
    pays = to_reps([pay] * reps)
    holds.append(hold(BACKWARD_WAVES[1], known, tiles, per_slot))
    packed, holds = lax.optimization_barrier((packed, holds))

    def products(wave, packed):
        sizes = BACKWARD_OUTPUTS[wave]
        first = wave * sum(sizes) // PAIR
        return list(
            backward_product(sizes, rows_dev, lists, first, packed, capacity, holds[wave], pays)
        )

    others = products(0, packed)
    packed, others[2] = lax.optimization_barrier((packed, others[2]))
    returned = swapped(others[0])
    sides = swapped(others[1])
    last = swapped(others[2])
    mine = products(1, packed)
    two = added(mine[2], returned[:rows_dev])
    ride = added(others[0][rows_dev:], returned[rows_dev:])
    from_below, from_above, later_order = lax.optimization_barrier(
        (
            up(jnp.concatenate([two[:half], ride])),
            down(jnp.concatenate([two[half:], ride])),
            node_order,
        )
    )
    near_order = moved(later_order, fetch_pairs())
    one = jnp.concatenate(
        [
            added(mine[1][:half], sides[:half], from_below[:half]),
            added(mine[1][half:], sides[half:rows_dev]),
            from_below[half:],
        ]
    )
    three = jnp.concatenate(
        [
            added(mine[3][:half], sides[rows_dev : rows_dev + half]),
            added(mine[3][half:], sides[rows_dev + half :], from_above[:half]),
        ]
    )
    below_sum, above_sum = up(one), down(three)
    ended = jnp.concatenate(
        [
            added(mine[0], last, below_sum[:rows_dev], above_sum),
            added(ride, from_below[half:], from_above[half:], below_sum[rows_dev:]),
        ]
    )
    quarters = restore(home_rep, near_order, ended, reps)
    terms = [moved(value, quarter_pairs(shift)) for shift, value in enumerate(quarters)]
    own = rows_dev // reps
    grad_features = added(*[term[:own] for term in terms])
    grad_weight = sum(term[own:].astype(jnp.float32) for term in terms)
    stacked = grad_weight.reshape(weight.shape[1] // TILE, weight.shape[0], TILE)
    grad_weight = jnp.concatenate([stacked[half] for half in range(stacked.shape[0])], axis=1)
    return (activations, grad_weight, grad_features)


def solution(mesh):
    placed = (
        P("blk", None),
        P("blk", None),
        P("blk", "rep", None, None, None, None),
        P("blk", "rep", None, None),
        P("blk", "rep", None, None),
        P("blk", "rep", None),
        P(),
        P(("blk", "rep"), None),
    )
    return jax.shard_map(
        per_device,
        mesh=mesh,
        in_specs=placed,
        out_specs=(P(("blk", "rep"), None), P(), P(("blk", "rep"), None)),
        check_vma=False,
    )
```
